256 devices in a mesh: ops: 32 (over y, x, core), sec: 8 (over z).
Axes of the slice: x: 4, y: 4, z: 8, core: 2. Of those that a mesh axis runs over, the one named last changes fastest.
Arguments:
- left_ops: bfloat16 [128, 16, 256, 256], P('ops', 'sec'), as said below
- right_ops: bfloat16 [128, 16, 256, 256], P('ops', 'sec'), as said below
- pattern: int32 [128, 16], P('ops', 'sec'), may hold values from 0 to 1, as said below
- guess_vector: float32 [16, 256, 256], P('sec'), may hold values from -6 to 6
- precond: float32 [16, 256, 256], P('sec'), may hold values from 0.5 to 8
- rotation: bfloat16 [16, 256, 256], P('sec', None, 'ops'), may hold values from -1.5 to 1.5
Outputs:
- new_state: float32 [16, 256, 256], P('sec', 'ops')
- energy: float32 [1], replicated
- renormalized: bfloat16 [128, 16, 256, 256], P('ops', 'sec')
The draws below stay inside these ranges and needn't reach their ends.
Inputs may be any that keep to these rules, and one draw needn't show every extreme that they name: pattern[k, s] is 1 where operator k has a block in sector s, else 0. Every block left_ops[k, s] is symmetric. Every block right_ops[k, s] is symmetric.
All inputs are finite; a program needn't handle non-finite values.
Results may differ from the reference program's by a relative error of at most 0.009.
Values may be sent and summed in bfloat16 or wider, within the bound.
No kernel may reach another device: no remote copies, remote signals or barrier semaphores. Data moves between devices by JAX's collectives and lax.ppermute only.
A program may use at most 64 MiB of HBM per device.

```python
import math
import jax
import jax.numpy as jnp
from jax import lax

B = 256
OPS = 128
NSEC = 16


def operator_blocks(key):
    key_gauss, key_level = jax.random.split(key, 2)
    gaussian = jax.random.normal(key_gauss, (OPS, NSEC, B, B), jnp.float32)
    symmetric = (gaussian + jnp.swapaxes(gaussian, 2, 3)) * 0.5 ** 0.5 / B ** 0.5
    levels = jax.random.uniform(key_level, (OPS, NSEC, 1, 1), jnp.float32, 0.5, 1.5)
    identity = (lax.broadcasted_iota(jnp.int32, (B, B), 0) == lax.broadcasted_iota(jnp.int32, (B, B), 1)).astype(jnp.float32)
    return symmetric + levels * identity


def draw_left_ops(key, part):
    blocks = operator_blocks(jax.random.fold_in(key, 11))
    return blocks.astype(jnp.bfloat16)


def draw_right_ops(key, part):
    blocks = operator_blocks(jax.random.fold_in(key, 21))
    return blocks.astype(jnp.bfloat16)


def draw_pattern(key, part):
    key_level, key_rolled = jax.random.split(jax.random.fold_in(key, 31), 2)
    levels = jax.random.randint(key_level, (OPS, 1), 1, 10)
    rolled = jax.random.randint(key_rolled, (OPS, NSEC), 0, 10)
    return (rolled < levels).astype(jnp.int32)


def block_scale(key, dims, pieces, smallest, high):
    factor_of, own = 1.0, jax.random.fold_in(key, 6)
    for dim, parts in pieces:
        heights = jnp.exp(jax.random.uniform(jax.random.fold_in(own, dim), (parts,), jnp.float32, smallest / len(pieces), high / len(pieces)))
        factor_of = factor_of * jnp.repeat(heights, dims[dim] // parts).reshape([-1 if axis == dim else 1 for axis in range(len(dims))])
    return factor_of


def scatter_about(rng, extent, deviation, bound, shards=(), kind=jnp.bfloat16):
    values = jax.random.normal(rng, extent, jnp.float32) * deviation
    if len(shards) > 0:
        values = block_scale(rng, extent, shards, -0.22, 0.18) * values
    return jnp.clip(values, min=-bound, max=bound).astype(kind)


def setup_inputs(seed: int = 0) -> dict:
    arg_keys = jax.random.split(jax.random.key(seed), 7)
    return {
        "left_ops": draw_left_ops(jax.random.fold_in(arg_keys[6], 71), 0),
        "right_ops": draw_right_ops(jax.random.fold_in(arg_keys[6], 71), 0),
        "pattern": draw_pattern(jax.random.fold_in(arg_keys[6], 71), 0),
        "guess_vector": scatter_about(arg_keys[3], (NSEC, B, B), 1.0, 6.0, ((0, 8),), jnp.float32),
        "precond": jnp.clip(jnp.exp(math.log(8.0) - 2.7725887 * jax.random.uniform(arg_keys[4], (NSEC, B, B), jnp.float32) ** block_scale(arg_keys[4], (NSEC, B, B), ((0, 8),), -0.2, 0.2)), 0.5, 8.0),
        "rotation": scatter_about(arg_keys[5], (NSEC, B, B), 0.25, 1.5, ((0, 8), (2, 32))),
    }


def apply_hamiltonian(vector, left_ops, right_ops, pattern):
    vec_low = vector.astype(jnp.bfloat16)

    def one_sector(sector):
        left_block = jnp.take(left_ops, sector, axis=1).astype(jnp.float32)
        right_block = jnp.take(right_ops, sector, axis=1).astype(jnp.float32)
        state_block = jnp.take(vec_low, sector, axis=0).astype(jnp.float32)
        halfway = jnp.einsum('kij,jl->kil', left_block, state_block).astype(jnp.bfloat16)
        active = jnp.take(pattern, sector, axis=1).astype(jnp.float32)
        return jnp.einsum('kil,kml->im', halfway.astype(jnp.float32) * active[:, None, None], right_block)
    return lax.map(one_sector, jnp.arange(NSEC, dtype=jnp.int32))

def reference(left_ops, right_ops, pattern, guess_vector, precond, rotation):
    first = guess_vector / jnp.sqrt(jnp.mean(guess_vector * guess_vector) + 1e-06)
    image_first = apply_hamiltonian(first, left_ops, right_ops, pattern)
    rayleigh_first = jnp.mean(first * image_first)
    correction = (image_first - rayleigh_first * first) / precond
    correlation = jnp.mean(first * correction)
    orthogonal = correction - correlation * first
    second = orthogonal / jnp.sqrt(jnp.mean(orthogonal * orthogonal) + 1e-06)
    image_second = apply_hamiltonian(second, left_ops, right_ops, pattern)
    coupling = jnp.mean(first * image_second)
    rayleigh_second = jnp.mean(second * image_second)
    half_gap = (rayleigh_first - rayleigh_second) / 2
    energy = (rayleigh_first + rayleigh_second) / 2 - jnp.sqrt(half_gap * half_gap + coupling * coupling)
    weight_first = rayleigh_second - energy
    weight_second = -coupling
    scaling = jnp.sqrt(weight_first * weight_first + weight_second * weight_second)
    new_state = (weight_first * first + weight_second * second) / scaling

    def renorm_sector(sector):
        left_block = jnp.take(left_ops, sector, axis=1).astype(jnp.float32)
        rotate = jnp.take(rotation, sector, axis=0).astype(jnp.float32)
        rotated = jnp.einsum('kij,jl->kil', left_block, rotate).astype(jnp.bfloat16)
        return jnp.einsum('ji,kjl->kil', rotate, rotated.astype(jnp.float32)).astype(jnp.bfloat16)
    renorm_all = lax.map(renorm_sector, jnp.arange(NSEC, dtype=jnp.int32))
    renormalized = jnp.swapaxes(renorm_all, 0, 1)
    return (new_state, jnp.reshape(energy, (1,)), renormalized)
```

```python
import jax
import jax.numpy as jnp
from jax import lax
from jax.experimental import pallas as pl
from jax.experimental.pallas import tpu as pltpu
from jax.sharding import Mesh, PartitionSpec as P

F32 = jnp.float32
BF16 = jnp.bfloat16
OPS = ("chip", "core")
VMEM = pl.BlockSpec(memory_space=pltpu.VMEM)
SMEM = pl.BlockSpec(memory_space=pltpu.SMEM)
HBM = pl.BlockSpec(memory_space=pltpu.HBM)


def dot(a, b):
    return jnp.dot(a, b, preferred_element_type=F32)


def sigma_block(s, x, pattern, left, right):
    total = None
    for k in range(left.shape[0]):
        half = (dot(left[k, s], x) * pattern[k, s].astype(F32)).astype(BF16)
        term = dot(half, right[k, s])
        total = term if total is None else total + term
    return total


def partial_kernel(pattern, left_hbm, right_hbm, guess_hbm, rot, out, left, right, guess, left_sem, right_sem, guess_sem):
    ops, sectors = left.shape[:2]
    copies = {}
    for s in range(sectors):
        copies["g", s] = pltpu.make_async_copy(guess_hbm.at[s], guess.at[s], guess_sem.at[s])
        copies["g", s].start()
        for k in range(ops):
            copies["l", k, s] = pltpu.make_async_copy(left_hbm.at[k, s], left.at[k, s], left_sem.at[k, s])
            copies["l", k, s].start()
        for k in range(ops):
            copies["r", k, s] = pltpu.make_async_copy(right_hbm.at[k, s], right.at[k, s], right_sem.at[k, s])
            copies["r", k, s].start()
    peers = out.shape[0]
    parts = []
    for s in range(sectors):
        copies["g", s].wait()
        x = guess[s].astype(BF16)
        halves = []
        for k in range(ops):
            copies["l", k, s].wait()
            halves.append((dot(left[k, s], x) * pattern[k, s].astype(F32)).astype(BF16))
        total = None
        for k in range(ops):
            copies["r", k, s].wait()
            term = dot(halves[k], right[k, s])
            total = term if total is None else total + term
        parts.append(total.reshape(peers, -1, total.shape[1]))
    turned = [jnp.transpose(rot[s].astype(F32)) for s in range(sectors)]
    columns = jnp.stack(turned)
    columns = jnp.broadcast_to(columns[None], (peers // sectors,) + columns.shape).reshape((peers,) + turned[0].shape)
    out[...] = jnp.concatenate(parts + [columns], axis=1).astype(BF16)


def level_kernel(pattern, left, right, guess, precond, out):
    total = None
    for s in range(guess.shape[0]):
        d = guess[s] / precond[s]
        image = sigma_block(s, d.astype(BF16), pattern, left, right)
        term = jnp.sum(d * image, axis=0, keepdims=True)
        total = term if total is None else total + term
    out[...] = total


def rows_kernel(received, guess, precond, image_out, scaled_out, chunks):
    sectors, rows = guess.shape[:2]
    image = jnp.sum(received[:, : sectors * rows, :].astype(F32), axis=0)
    scaled = image / precond[...].reshape(image.shape)
    image_out[...] = image.reshape(guess.shape)
    scaled_out[...] = scaled.reshape(guess.shape)
    chunks[...] = jnp.broadcast_to(scaled[None].astype(BF16), chunks.shape)


def row_sums_kernel(guess, precond, image, scaled, sums):
    g, h, y = guess[...], image[...], scaled[...]
    d = g / precond[...]
    pairs = ((g, g), (g, h), (g, d), (d, d), (g, y), (d, y), (y, y), (h, y))
    sums[...] = jnp.concatenate([jnp.sum(a * b, axis=(0, 1)).reshape(1, -1) for a, b in pairs], axis=0)


def columns_kernel(received, out):
    width = received.shape[2]
    out[...] = received[:, received.shape[1] - width // received.shape[0] :, :].astype(F32).reshape(width, width).astype(BF16)


def renorm_kernel(core, left, mine, theirs, out):
    first = (core[0] == 0).astype(F32)
    a, b = mine[...].astype(F32), theirs[...].astype(F32)
    for s in range(left.shape[1]):
        turned = a * first + b * (1.0 - first) if s == 0 else b * first + a * (1.0 - first)
        rotation = jnp.transpose(turned).astype(BF16)
        turned = turned.astype(BF16)
        for k in range(left.shape[0]):
            rotated = dot(left[k, s], rotation).astype(BF16)
            out[k, s] = dot(turned, rotated).astype(BF16)


def second_kernel(pattern, received, left, right, guess, precond, row_sums, level, out):
    sectors, states = guess.shape[:2]
    rows = states // received.shape[0]
    y_hy, d_hy = None, None
    for s in range(sectors):
        y = received[:, s * rows : (s + 1) * rows, :].astype(F32).reshape(states, states)
        image = sigma_block(s, y.astype(BF16), pattern, left, right)
        d = guess[s] / precond[s]
        a, b = jnp.sum(y * image, axis=0, keepdims=True), jnp.sum(d * image, axis=0, keepdims=True)
        y_hy, d_hy = (a, b) if y_hy is None else (y_hy + a, d_hy + b)
    low = jnp.sum(row_sums[...], axis=1, keepdims=True)
    high = jnp.concatenate([y_hy, d_hy, level[...], jnp.zeros((5, states), F32)], axis=0)
    high = jnp.sum(high, axis=1, keepdims=True)
    lane = lax.broadcasted_iota(jnp.int32, out.shape[1:], 1)
    tile = jnp.where(lane == 0, low, jnp.where(lane == 1, high, 0.0))
    out[...] = jnp.broadcast_to(tile[None], out.shape)


def gather_kernel(received, out):
    total = jnp.sum(received[...], axis=0)
    out[...] = jnp.broadcast_to(total[None], out.shape)


def state_kernel(entries, received, guess, precond, scaled, state, energy_out):
    sums = jnp.sum(received[...], axis=0)
    lane = lax.broadcasted_iota(jnp.int32, sums.shape, 1)
    low = jnp.sum(jnp.where(lane == 0, sums, 0.0), axis=1, keepdims=True)
    high = jnp.sum(jnp.where(lane == 1, sums, 0.0), axis=1, keepdims=True)
    gg, gh, gd, dd, gy, dy, yy, hy = [low[i : i + 1] for i in range(8)]
    y_hy, d_hy, d_hd = [high[i : i + 1] for i in range(3)]
    inverse = 1.0 / entries
    first_square = 1.0 / (gg * inverse + 1e-06)
    rho = first_square * gh * inverse
    kappa = first_square * (gy - rho * gd) * inverse
    qq = yy - 2.0 * rho * dy + rho * rho * dd - 2.0 * kappa * (gy - rho * gd) + kappa * kappa * gg
    hq = hy - rho * gy - kappa * gh
    q_hq = y_hy - 2.0 * rho * d_hy + rho * rho * d_hd - 2.0 * kappa * (hy - rho * gy) + kappa * kappa * gh
    second_square = 1.0 / (first_square * qq * inverse + 1e-06)
    second_scale = jnp.sqrt(second_square)
    first_scale = jnp.sqrt(first_square)
    coupling = second_scale * first_square * hq * inverse
    rho_second = second_square * first_square * q_hq * inverse
    half_gap = (rho - rho_second) * 0.5
    energy = (rho + rho_second) * 0.5 - jnp.sqrt(half_gap * half_gap + coupling * coupling)
    weight_first = rho_second - energy
    weight_second = -coupling
    scaling = 1.0 / jnp.sqrt(weight_first * weight_first + weight_second * weight_second)
    on_second = weight_second * second_scale * scaling * first_scale
    on_first = weight_first * scaling * first_scale
    energy_out[...] = jnp.broadcast_to(energy, energy_out.shape)
    g = guess[...]
    d = g / precond[...]
    state[...] = on_first[None] * g + on_second[None] * (scaled[...] - rho[None] * d - kappa[None] * g)


def call(kernel, out_shape, in_specs, flops=0, scratch=(), out_specs=VMEM):
    return pl.pallas_call(
        kernel,
        out_shape=out_shape,
        in_specs=in_specs,
        out_specs=jax.tree.map(lambda _: out_specs, out_shape),
        scratch_shapes=scratch,
        cost_estimate=pl.CostEstimate(flops=flops, bytes_accessed=1 << 20, transcendentals=0),
        compiler_params=pltpu.CompilerParams(vmem_limit_bytes=16 << 20),
    )


def local(left, right, pattern, guess, precond, rotation):
    ops, sectors, states = left.shape[:3]
    peers = lax.axis_size(OPS)
    zones = lax.axis_size("sec")
    rows = states // peers
    me = lax.axis_index(OPS)
    entries = float(sectors * zones * states * states)
    shape = jax.ShapeDtypeStruct
    flops = 4 * ops * sectors * states**3

    parts = call(
        partial_kernel,
        shape((peers, (sectors + 1) * rows, states), BF16),
        [SMEM, HBM, HBM, HBM, VMEM],
        flops,
        [
            pltpu.VMEM(left.shape, BF16),
            pltpu.VMEM(right.shape, BF16),
            pltpu.VMEM(guess.shape, F32),
            pltpu.SemaphoreType.DMA((ops, sectors)),
            pltpu.SemaphoreType.DMA((ops, sectors)),
            pltpu.SemaphoreType.DMA((sectors,)),
        ],
    )(pattern, left, right, guess, rotation)
    received = lax.all_to_all(parts, OPS, 0, 0)

    level = call(level_kernel, shape((1, states), F32), [SMEM] + [VMEM] * 4, flops)(pattern, left, right, guess, precond)
    guess_rows = lax.dynamic_slice_in_dim(guess, me * rows, rows, 1)
    precond_rows = lax.dynamic_slice_in_dim(precond, me * rows, rows, 1)

    block = shape(guess_rows.shape, F32)
    image_rows, scaled_rows, chunks = call(
        rows_kernel, (block, block, shape((peers, sectors * rows, states), BF16)), [VMEM] * 3
    )(received, guess_rows, precond_rows)
    gathered = lax.all_to_all(chunks, OPS, 0, 0)

    mine = call(columns_kernel, shape((states, states), BF16), [VMEM])(received)
    theirs = lax.ppermute(mine, "core", [(0, 1), (1, 0)])
    row_sums = call(row_sums_kernel, shape((8, states), F32), [VMEM] * 4)(
        guess_rows, precond_rows, image_rows, scaled_rows
    )
    core = lax.axis_index("core").reshape(1)
    renormalized = call(renorm_kernel, shape(left.shape, BF16), [SMEM, VMEM, VMEM, VMEM], flops)(
        core, left, mine, theirs
    )

    sums = call(second_kernel, shape((peers, 8, 128), F32), [SMEM] + [VMEM] * 7, flops)(
        pattern, gathered, left, right, guess, precond, row_sums, level
    )
    sums = lax.all_to_all(sums, OPS, 0, 0)
    sums = call(gather_kernel, shape((zones, 8, 128), F32), [VMEM])(sums)
    sums = lax.all_to_all(sums, "sec", 0, 0)
    new_state, energy = call(
        lambda *refs: state_kernel(entries, *refs), (block, shape((1, 128), F32)), [VMEM] * 4
    )(sums, guess_rows, precond_rows, scaled_rows)
    return new_state, energy[0, :1], renormalized


def solution(mesh):
    cores = 2
    mesh = Mesh(mesh.devices.reshape(-1, cores, mesh.shape["sec"]), ("chip", "core", "sec"))
    return jax.shard_map(
        local,
        mesh=mesh,
        in_specs=(
            P(OPS, "sec", None, None),
            P(OPS, "sec", None, None),
            P(OPS, "sec"),
            P("sec", None, None),
            P("sec", None, None),
            P("sec", None, OPS),
        ),
        out_specs=(P("sec", OPS, None), P(), P(OPS, "sec", None, None)),
        check_vma=False,
    )
```

```python
import jax
import jax.numpy as jnp
from jax import lax
from jax.experimental import pallas as pl
from jax.experimental.pallas import tpu as pltpu
from jax.sharding import Mesh, PartitionSpec as P

F32 = jnp.float32
BF16 = jnp.bfloat16
OPS = ("chip", "core")
VMEM = pl.BlockSpec(memory_space=pltpu.VMEM)
SMEM = pl.BlockSpec(memory_space=pltpu.SMEM)
HBM = pl.BlockSpec(memory_space=pltpu.HBM)


def dot(a, b):
    return jnp.dot(a, b, preferred_element_type=F32)


def total_of(terms):
    total = terms[0]
    for term in terms[1:]:
        total = total + term
    return total


def partial_kernel(
    pattern, me, left_hbm, right_hbm, guess_hbm, precond_hbm, rot,
    chunks, left, right, level, rows_out,
    guess, precond, left_sem, right_sem, guess_sem, precond_sem,
):
    ops, sectors = left.shape[:2]
    peers = chunks.shape[0]
    rows = guess.shape[1] // peers
    copies = {}

    def start(name, source, target, sem):
        copies[name] = pltpu.make_async_copy(source, target, sem)
        copies[name].start()

    for s in range(sectors):
        start(("g", s), guess_hbm.at[s], guess.at[s], guess_sem.at[s])
        for k in range(ops):
            start(("l", k, s), left_hbm.at[k, s], left.at[k, s], left_sem.at[k, s])
        for k in range(ops):
            start(("r", k, s), right_hbm.at[k, s], right.at[k, s], right_sem.at[k, s])
    for s in range(sectors):
        start(("p", s), precond_hbm.at[s], precond.at[s], precond_sem.at[s])
    parts = []
    for s in range(sectors):
        copies["g", s].wait()
        g = guess[s]
        high = g.astype(BF16)
        low = (g - high.astype(F32)).astype(BF16)
        halves = []
        for k in range(ops):
            copies["l", k, s].wait()
            half = dot(left[k, s], high) + dot(left[k, s], low)
            halves.append((half * pattern[s, k].astype(F32)).astype(BF16))
        terms = []
        for k in range(ops):
            copies["r", k, s].wait()
            terms.append(dot(halves[k], right[k, s]))
        parts.append(total_of(terms).reshape(peers, rows, g.shape[1]))
    columns = rot[...].astype(F32)
    columns = jnp.broadcast_to(columns[None], (peers // sectors,) + columns.shape).reshape((peers,) + columns.shape[1:])
    chunks[...] = jnp.concatenate(parts + [columns], axis=1).astype(BF16)
    own = pl.ds(pl.multiple_of(me[0] * rows, rows), rows)
    for s in range(sectors):
        copies["p", s].wait()
        level[s] = guess[s] / precond[s]
        rows_out[0, s] = guess[s, own, :]
        rows_out[1, s] = level[s, own, :]
        rows_out[2, s] = precond[s, own, :]


def rows_kernel(received, rows_in, kept, chunks):
    g, d, p = rows_in[0], rows_in[1], rows_in[2]
    sectors, rows, states = g.shape
    image = jnp.sum(received[:, : sectors * rows, :].astype(F32), axis=0)
    h = image.reshape(g.shape)
    y = h / p
    pairs = ((g, g), (g, h), (g, d), (d, d), (g, y), (d, y), (y, y), (h, y))
    sums = jnp.concatenate([jnp.sum(a * b, axis=(0, 1)).reshape(1, -1) for a, b in pairs], axis=0)
    kept[...] = jnp.concatenate([y.reshape(-1, states), sums], axis=0)
    chunks[...] = jnp.broadcast_to(y.reshape(1, -1, states).astype(BF16), chunks.shape)


def second_kernel(pattern, received, left, right, level, kept, out):
    ops, sectors, states = left.shape[:3]
    rows = states // received.shape[0]
    y_hy, d_hy, d_hd = [], [], []
    for s in range(sectors):
        d = level[s]
        y = received[:, s * rows : (s + 1) * rows, :].astype(F32).reshape(states, states)
        low = jnp.concatenate([y.astype(BF16), d.astype(BF16)], axis=1)
        terms = []
        for k in range(ops):
            half = (dot(left[k, s], low) * pattern[s, k].astype(F32)).astype(BF16)
            half = jnp.concatenate([half[:, :states], half[:, states:]], axis=0)
            terms.append(dot(half, right[k, s]))
        image = total_of(terms)
        y_hy.append(jnp.sum(y * image[:states], axis=0, keepdims=True))
        d_hy.append(jnp.sum(d * image[:states], axis=0, keepdims=True))
        d_hd.append(jnp.sum(d * image[states:], axis=0, keepdims=True))
    low = jnp.sum(kept[sectors * rows :, :], axis=1, keepdims=True)
    high = jnp.concatenate([total_of(y_hy), total_of(d_hy), total_of(d_hd), jnp.zeros((5, states), F32)], axis=0)
    high = jnp.sum(high, axis=1, keepdims=True)
    lane = lax.broadcasted_iota(jnp.int32, out.shape[1:], 1)
    tile = jnp.where(lane == 0, low, jnp.where(lane == 1, high, 0.0))
    out[...] = jnp.broadcast_to(tile[None], out.shape)


def gather_kernel(received, out):
    out[...] = jnp.broadcast_to(jnp.sum(received[...], axis=0)[None], out.shape)


def columns_kernel(received, after, out):
    del after
    width = received.shape[2]
    out[...] = received[:, received.shape[1] - width // received.shape[0] :, :].astype(F32).reshape(width, width).astype(BF16)


def renorm_kernel(core, left, mine, theirs, out):
    first = (core[0] == 0).astype(F32)
    a, b = mine[...].astype(F32), theirs[...].astype(F32)
    for s in range(left.shape[1]):
        turned = a * first + b * (1.0 - first) if s == 0 else b * first + a * (1.0 - first)
        rotation = jnp.transpose(turned).astype(BF16)
        turned = turned.astype(BF16)
        for k in range(left.shape[0]):
            rotated = dot(left[k, s], rotation).astype(BF16)
            out[k, s] = dot(turned, rotated).astype(BF16)


def state_kernel(entries, received, rows_in, kept, state, energy_out):
    sums = jnp.sum(received[...], axis=0)
    lane = lax.broadcasted_iota(jnp.int32, sums.shape, 1)
    low = jnp.sum(jnp.where(lane == 0, sums, 0.0), axis=1, keepdims=True)
    high = jnp.sum(jnp.where(lane == 1, sums, 0.0), axis=1, keepdims=True)
    gg, gh, gd, dd, gy, dy, yy, hy = [low[i : i + 1] for i in range(8)]
    y_hy, d_hy, d_hd = [high[i : i + 1] for i in range(3)]
    inverse = 1.0 / entries
    first_square = 1.0 / (gg * inverse + 1e-06)
    rho = first_square * gh * inverse
    kappa = first_square * (gy - rho * gd) * inverse
    qq = yy - 2.0 * rho * dy + rho * rho * dd - 2.0 * kappa * (gy - rho * gd) + kappa * kappa * gg
    hq = hy - rho * gy - kappa * gh
    q_hq = y_hy - 2.0 * rho * d_hy + rho * rho * d_hd - 2.0 * kappa * (hy - rho * gy) + kappa * kappa * gh
    second_square = 1.0 / (first_square * qq * inverse + 1e-06)
    second_scale = jnp.sqrt(second_square)
    first_scale = jnp.sqrt(first_square)
    coupling = second_scale * first_square * hq * inverse
    rho_second = second_square * first_square * q_hq * inverse
    half_gap = (rho - rho_second) * 0.5
    energy = (rho + rho_second) * 0.5 - jnp.sqrt(half_gap * half_gap + coupling * coupling)
    weight_first = rho_second - energy
    weight_second = -coupling
    scaling = 1.0 / jnp.sqrt(weight_first * weight_first + weight_second * weight_second)
    on_second = weight_second * second_scale * scaling * first_scale
    on_first = weight_first * scaling * first_scale
    energy_out[...] = jnp.broadcast_to(energy, energy_out.shape)
    g, d = rows_in[0], rows_in[1]
    y = kept[: g.shape[0] * g.shape[1], :].reshape(g.shape)
    state[...] = on_first[None] * g + on_second[None] * (y - rho[None] * d - kappa[None] * g)


def call(kernel, out_shape, in_specs, flops=0, scratch=(), limit=16):
    return pl.pallas_call(
        kernel,
        out_shape=out_shape,
        in_specs=in_specs,
        out_specs=jax.tree.map(lambda _: VMEM, out_shape),
        scratch_shapes=scratch,
        cost_estimate=pl.CostEstimate(flops=flops, bytes_accessed=1 << 20, transcendentals=0),
        compiler_params=pltpu.CompilerParams(vmem_limit_bytes=limit << 20),
    )


def local(left_hbm, right_hbm, pattern, guess, precond, rotation):
    ops, sectors, states = left_hbm.shape[:3]
    chips, cores, zones = (lax.axis_size(axis) for axis in ("chip", "core", "sec"))
    peers = chips * cores
    rows = states // peers
    me = lax.axis_index(OPS).reshape(1)
    core = lax.axis_index("core").reshape(1)
    entries = float(sectors * zones * states * states)
    shape = jax.ShapeDtypeStruct
    flops = 4 * ops * sectors * states**3
    pattern = jnp.swapaxes(pattern, 0, 1)
    columns = jnp.swapaxes(rotation, 1, 2)

    def in_hbm(x):
        return pltpu.with_memory_space_constraint(x, pltpu.HBM)

    chunks, left, right, level, own = call(
        partial_kernel,
        (
            shape((peers, (sectors + 1) * rows, states), BF16),
            shape(left_hbm.shape, BF16),
            shape(right_hbm.shape, BF16),
            shape(guess.shape, F32),
            shape((3, sectors, rows, states), F32),
        ),
        [SMEM, SMEM, HBM, HBM, HBM, HBM, VMEM],
        flops,
        [
            pltpu.VMEM(guess.shape, F32),
            pltpu.VMEM(guess.shape, F32),
            pltpu.SemaphoreType.DMA((ops, sectors)),
            pltpu.SemaphoreType.DMA((ops, sectors)),
            pltpu.SemaphoreType.DMA((sectors,)),
            pltpu.SemaphoreType.DMA((sectors,)),
        ],
    )(pattern, me, in_hbm(left_hbm), in_hbm(right_hbm), in_hbm(guess), in_hbm(precond), columns)
    received = lax.all_to_all(chunks, OPS, 0, 0)
    kept, chunks = call(
        rows_kernel,
        (shape(((sectors + 1) * rows, states), F32), shape((peers, sectors * rows, states), BF16)),
        [VMEM] * 2,
    )(received, own)
    gathered = lax.all_to_all(chunks, OPS, 0, 0)
    sums = call(second_kernel, shape((chips, 8, 128), F32), [SMEM] + [VMEM] * 5, 2 * flops)(
        pattern, gathered, left, right, level, kept
    )
    over_chips = lax.all_to_all(sums, "chip", 0, 0)
    sums = call(gather_kernel, shape((cores * zones, 8, 128), F32), [VMEM])(over_chips)
    sums = lax.all_to_all(sums, ("core", "sec"), 0, 0)

    mine = call(columns_kernel, shape((states, states), BF16), [VMEM] * 2)(received, over_chips)
    theirs = lax.ppermute(mine, "core", [(0, 1), (1, 0)])
    renormalized = call(renorm_kernel, shape(left.shape, BF16), [SMEM, VMEM, VMEM, VMEM], flops)(
        core, left, mine, theirs
    )
    new_state, energy = call(
        lambda *refs: state_kernel(entries, *refs),
        (shape((sectors, rows, states), F32), shape((1, 128), F32)),
        [VMEM] * 3,
    )(sums, own, kept)
    return new_state, energy[0, :1], renormalized


def solution(mesh):
    cores = 2
    mesh = Mesh(mesh.devices.reshape(-1, cores, mesh.shape["sec"]), ("chip", "core", "sec"))
    return jax.shard_map(
        local,
        mesh=mesh,
        in_specs=(
            P(OPS, "sec", None, None),
            P(OPS, "sec", None, None),
            P(OPS, "sec"),
            P("sec", None, None),
            P("sec", None, None),
            P("sec", None, OPS),
        ),
        out_specs=(P("sec", OPS, None), P(), P(OPS, "sec", None, None)),
        check_vma=False,
    )
```

```python
import jax
import jax.numpy as jnp
from jax import lax
from jax.experimental import pallas as pl
from jax.experimental.pallas import tpu as pltpu
from jax.sharding import Mesh, PartitionSpec as P

F32 = jnp.float32
BF16 = jnp.bfloat16
OPS = ("chip", "core")
SWAP = [(0, 1), (1, 0)]
VMEM = pl.BlockSpec(memory_space=pltpu.VMEM)
SMEM = pl.BlockSpec(memory_space=pltpu.SMEM)
HBM = pl.BlockSpec(memory_space=pltpu.HBM)


def dot(a, b):
    return jnp.dot(a, b, preferred_element_type=F32)


def halves_of(left, s, flags, x):
    terms = x.shape[0] // left.shape[3]
    halves = []
    for k in range(left.shape[0]):
        block = left[k, s]
        half = dot(jnp.concatenate([block] * terms, axis=1), x)
        halves.append(half.astype(BF16) * flags(s, k))
    return halves


def in_rows(ref):
    return lambda s, k: ref[s, pl.ds(k, 1), :].astype(BF16)


def closed(halves, right, s):
    return dot(jnp.concatenate(halves, axis=1), right[:, s].reshape(-1, right.shape[3]))


def two_terms(x):
    high = x.astype(BF16)
    return jnp.concatenate([high, (x - high.astype(F32)).astype(BF16)], axis=0)


def other_kernel(
    core, chip, pattern_hbm, left_hbm, right_hbm, guess_hbm,
    part, left, right, guess, flags,
    pattern, pattern_sem, guess_sem, left_sem, right_sem,
):
    del chip
    mine = core[0]
    other = 1 - mine
    first = pltpu.make_async_copy(pattern_hbm, pattern, pattern_sem)
    first.start()
    copies = []
    for i, s in enumerate((other, mine)):
        copies.append(
            [
                pltpu.make_async_copy(guess_hbm.at[s], guess.at[s], guess_sem.at[i]),
                pltpu.make_async_copy(left_hbm.at[:, s], left.at[:, s], left_sem.at[i]),
                pltpu.make_async_copy(right_hbm.at[:, s], right.at[:, s], right_sem.at[i]),
            ]
        )
        for copy in copies[i]:
            copy.start()
    first.wait()
    for s in range(left.shape[1]):
        for k in range(left.shape[0]):
            flags[s, pl.ds(k, 1), :] = jnp.full((1, flags.shape[2]), pattern[s, k].astype(F32))
    copies[0][0].wait()
    copies[0][1].wait()
    halves = halves_of(left, other, in_rows(flags), two_terms(guess[other]))
    copies[0][2].wait()
    part[...] = closed(halves, right, other).astype(BF16)
    for copy in copies[1]:
        copy.wait()


def own_kernel(core, chip, flags, left, right, guess, precond_hbm, part, level, rows_out, state_rows, precond, precond_sem):
    mine = core[0]
    copy = pltpu.make_async_copy(precond_hbm, precond, precond_sem)
    copy.start()
    part[...] = closed(halves_of(left, mine, in_rows(flags), two_terms(guess[mine])), right, mine)
    copy.wait()
    level[...] = guess[...] / precond[...]
    count = rows_out.shape[1]
    own = pl.ds(pl.multiple_of(chip[0] * count, count), count)
    for i, ref in enumerate((guess, level, precond)):
        rows_out[i] = ref[mine, own, :]
    count = state_rows.shape[2]
    own = pl.ds(pl.multiple_of((chip[0] * 2 + mine) * count, count), count)
    for i, ref in enumerate((guess, level)):
        for s in range(ref.shape[0]):
            state_rows[i, s] = ref[s, own, :]


def chunks_kernel(core, own, theirs, columns, columns_theirs, chunks):
    mine = core[0]
    total = own[...] + theirs[...].astype(F32)
    a, b = columns[mine].astype(F32), columns_theirs[mine].astype(F32)
    first = (mine == 0).astype(F32)
    turned = jnp.concatenate([a * first + b * (1.0 - first), b * first + a * (1.0 - first)], axis=0)
    chips, count, states = chunks.shape
    turned = jnp.broadcast_to(turned[None], (chips,) + turned.shape)
    chunks[...] = jnp.concatenate([total.reshape(chips, -1, states), turned], axis=1).astype(BF16)


def rows_kernel(received, rows_in, kept, sums, rotation, chunks):
    g, d, p = rows_in[0], rows_in[1], rows_in[2]
    count, states = g.shape
    h = jnp.sum(received[:, :count, :].astype(F32), axis=0)
    rotation[...] = received[:, count:, :].reshape(states, states)
    y = h / p
    pairs = ((g, g), (g, h), (g, d), (d, d), (g, y), (d, y), (y, y), (h, y))
    sums[...] = jnp.concatenate([jnp.sum(a * b, axis=0, keepdims=True) for a, b in pairs], axis=0)
    kept[...] = y
    chunks[...] = jnp.broadcast_to(y[None].astype(BF16), chunks.shape)


def renorm_kernel(core, flags, left, right, level, mine, theirs, kept, kept_theirs, out, d_hd, state_y):
    count = state_y.shape[1]
    own = pl.ds(pl.multiple_of(core[0] * count, count), count)
    state_y[core[0]] = kept[own, :]
    state_y[1 - core[0]] = kept_theirs[own, :]
    first = (core[0] == 0).astype(F32)
    a, b = mine[...].astype(F32), theirs[...].astype(F32)
    dots = []
    for s in range(left.shape[1]):
        turned = a * first + b * (1.0 - first) if s == 0 else b * first + a * (1.0 - first)
        rotation = jnp.transpose(turned).astype(BF16)
        turned = turned.astype(BF16)
        for k in range(left.shape[0]):
            rotated = dot(left[k, s], rotation).astype(BF16)
            out[k, s] = dot(turned, rotated).astype(BF16)
        d = level[s]
        image = closed(halves_of(left, s, in_rows(flags), d.astype(BF16)), right, s)
        dots.append(jnp.sum(d * image, axis=0, keepdims=True))
    d_hd[...] = dots[0] + dots[1]


def dots_of(s, flags, y, left, right, level):
    image = closed(halves_of(left, s, in_rows(flags), y), right, s)
    y_hy = jnp.sum(y.astype(F32) * image, axis=0, keepdims=True)
    d_hy = jnp.sum(level[s] * image, axis=0, keepdims=True)
    return jnp.concatenate([y_hy, d_hy], axis=0)


def own_dots_kernel(core, flags, gathered, left, right, level, d_hd, out):
    y = gathered[...].reshape(left.shape[2:])
    out[...] = jnp.concatenate([dots_of(core[0], flags, y, left, right, level), d_hd[...]], axis=0)


def other_dots_kernel(core, flags, gathered, left, right, level, own_dots, row_sums, out):
    y = gathered[...].reshape(left.shape[2:])
    dots = dots_of(1 - core[0], flags, y, left, right, level)
    low = jnp.sum(row_sums[...], axis=1, keepdims=True)
    high = jnp.concatenate([own_dots[...], dots, jnp.zeros((3, y.shape[1]), F32)], axis=0)
    high = jnp.sum(high, axis=1, keepdims=True)
    lane = lax.broadcasted_iota(jnp.int32, out.shape[1:], 1)
    tile = jnp.where(lane == 0, low, jnp.where(lane == 1, high, 0.0))
    out[...] = jnp.broadcast_to(tile[None], out.shape)


def gather_kernel(received, out):
    out[...] = jnp.broadcast_to(jnp.sum(received[...], axis=0)[None], out.shape)


def state_kernel(entries, received, state_rows, state_y, state, energy_out):
    sums = jnp.sum(received[...], axis=0)
    lane = lax.broadcasted_iota(jnp.int32, sums.shape, 1)
    low = jnp.sum(jnp.where(lane == 0, sums, 0.0), axis=1, keepdims=True)
    high = jnp.sum(jnp.where(lane == 1, sums, 0.0), axis=1, keepdims=True)
    gg, gh, gd, dd, gy, dy, yy, hy = [low[i : i + 1] for i in range(8)]
    y_hy, d_hy, d_hd = high[0:1] + high[3:4], high[1:2] + high[4:5], high[2:3]
    inverse = 1.0 / entries
    first_square = 1.0 / (gg * inverse + 1e-06)
    rho = first_square * gh * inverse
    kappa = first_square * (gy - rho * gd) * inverse
    qq = yy - 2.0 * rho * dy + rho * rho * dd - 2.0 * kappa * (gy - rho * gd) + kappa * kappa * gg
    hq = hy - rho * gy - kappa * gh
    q_hq = y_hy - 2.0 * rho * d_hy + rho * rho * d_hd - 2.0 * kappa * (hy - rho * gy) + kappa * kappa * gh
    second_square = 1.0 / (first_square * qq * inverse + 1e-06)
    second_scale = jnp.sqrt(second_square)
    first_scale = jnp.sqrt(first_square)
    coupling = second_scale * first_square * hq * inverse
    rho_second = second_square * first_square * q_hq * inverse
    half_gap = (rho - rho_second) * 0.5
    energy = (rho + rho_second) * 0.5 - jnp.sqrt(half_gap * half_gap + coupling * coupling)
    weight_first = rho_second - energy
    weight_second = -coupling
    scaling = 1.0 / jnp.sqrt(weight_first * weight_first + weight_second * weight_second)
    on_second = weight_second * second_scale * scaling * first_scale
    on_first = weight_first * scaling * first_scale
    energy_out[...] = jnp.broadcast_to(energy, energy_out.shape)
    g, d, y = state_rows[0], state_rows[1], state_y[...]
    state[...] = on_first[None] * g + on_second[None] * (y - rho[None] * d - kappa[None] * g)


def call(kernel, out_shape, in_specs, flops=0, scratch=(), limit=16):
    return pl.pallas_call(
        kernel,
        out_shape=out_shape,
        in_specs=in_specs,
        out_specs=jax.tree.map(lambda _: VMEM, out_shape),
        scratch_shapes=scratch,
        cost_estimate=pl.CostEstimate(flops=flops, bytes_accessed=1 << 20, transcendentals=0),
        compiler_params=pltpu.CompilerParams(vmem_limit_bytes=limit << 20),
    )


def local(left_hbm, right_hbm, pattern, guess_hbm, precond_hbm, rotation):
    ops, sectors, states = left_hbm.shape[:3]
    chips, cores, zones = (lax.axis_size(axis) for axis in ("chip", "core", "sec"))
    count = states // chips
    core = lax.axis_index("core").reshape(1)
    chip = lax.axis_index("chip").reshape(1)
    entries = float(sectors * zones * states * states)
    shape = jax.ShapeDtypeStruct
    dma = pltpu.SemaphoreType.DMA
    block = (states, states)
    flops = 4 * ops * sectors * states**3
    pattern = jnp.swapaxes(pattern, 0, 1)
    columns = jnp.swapaxes(rotation, 1, 2)

    def in_hbm(x):
        return pltpu.with_memory_space_constraint(x, pltpu.HBM)

    def swapped(x):
        return lax.ppermute(x, "core", SWAP)

    columns_theirs = swapped(columns)
    part, left, right, guess, flags = call(
        other_kernel,
        (
            shape(block, BF16),
            shape(left_hbm.shape, BF16),
            shape(right_hbm.shape, BF16),
            shape(guess_hbm.shape, F32),
            shape((sectors, ops, states), F32),
        ),
        [SMEM] * 2 + [HBM] * 4,
        flops // 2,
        [pltpu.SMEM(pattern.shape, jnp.int32), dma, dma((2,)), dma((2,)), dma((2,))],
    )(core, chip, *(in_hbm(x) for x in (pattern, left_hbm, right_hbm, guess_hbm)))
    theirs = swapped(part)
    own, level, own_rows, state_rows = call(
        own_kernel,
        (
            shape(block, F32),
            shape(guess.shape, F32),
            shape((3, count, states), F32),
            shape((2, sectors, count // cores, states), F32),
        ),
        [SMEM] * 2 + [VMEM] * 4 + [HBM],
        flops // 2,
        [pltpu.VMEM(guess.shape, F32), dma],
    )(core, chip, flags, left, right, guess, in_hbm(precond_hbm))
    chunks = call(chunks_kernel, shape((chips, 2 * count, states), BF16), [SMEM] + [VMEM] * 4)(
        core, own, theirs, columns, columns_theirs
    )
    received = lax.all_to_all(chunks, "chip", 0, 0)
    kept, row_sums, mine, chunks = call(
        rows_kernel,
        (
            shape((count, states), F32),
            shape((8, states), F32),
            shape(block, BF16),
            shape((chips, count, states), BF16),
        ),
        [VMEM] * 2,
    )(received, own_rows)
    gathered = lax.all_to_all(chunks, "chip", 0, 0)
    renormalized, d_hd, state_y = call(
        renorm_kernel,
        (shape(left.shape, BF16), shape((1, states), F32), shape((sectors, count // cores, states), F32)),
        [SMEM] + [VMEM] * 8,
        2 * flops,
    )(core, flags, left, right, level, mine, swapped(mine), kept, swapped(kept))
    gathered, d_hd = lax.optimization_barrier((gathered, d_hd))
    gathered_theirs = swapped(gathered)
    dots = call(own_dots_kernel, shape((3, states), F32), [SMEM] + [VMEM] * 6, flops // 2)(
        core, flags, gathered, left, right, level, d_hd
    )
    sums = call(other_dots_kernel, shape((chips, 8, 128), F32), [SMEM] + [VMEM] * 7, flops // 2)(
        core, flags, gathered_theirs, left, right, level, dots, row_sums
    )
    sums = lax.all_to_all(sums, "chip", 0, 0)
    sums = call(gather_kernel, shape((cores * zones, 8, 128), F32), [VMEM])(sums)
    sums = lax.all_to_all(sums, ("core", "sec"), 0, 0)
    new_state, energy = call(
        lambda *refs: state_kernel(entries, *refs),
        (shape((sectors, count // cores, states), F32), shape((1, 128), F32)),
        [VMEM] * 3,
    )(sums, state_rows, state_y)
    return new_state, energy[0, :1], renormalized


def solution(mesh):
    cores = 2
    mesh = Mesh(mesh.devices.reshape(-1, cores, mesh.shape["sec"]), ("chip", "core", "sec"))
    return jax.shard_map(
        local,
        mesh=mesh,
        in_specs=(
            P(OPS, "sec", None, None),
            P(OPS, "sec", None, None),
            P(OPS, "sec"),
            P("sec", None, None),
            P("sec", None, None),
            P("sec", None, OPS),
        ),
        out_specs=(P("sec", OPS, None), P(), P(OPS, "sec", None, None)),
        check_vma=False,
    )
```

```python
import jax
import jax.numpy as jnp
from jax import lax
from jax.experimental import pallas as pl
from jax.experimental.pallas import tpu as pltpu
from jax.sharding import Mesh, PartitionSpec as P

F32 = jnp.float32
BF16 = jnp.bfloat16
OPS = ("chip", "core")
SWAP = [(0, 1), (1, 0)]
VMEM = pl.BlockSpec(memory_space=pltpu.VMEM)
SMEM = pl.BlockSpec(memory_space=pltpu.SMEM)
HBM = pl.BlockSpec(memory_space=pltpu.HBM)


def dot(a, b):
    return jnp.dot(a, b, preferred_element_type=F32)


def halves_of(left, s, flags, x):
    terms = x.shape[0] // left.shape[3]
    halves = []
    for k in range(left.shape[0]):
        block = left[k, s]
        half = dot(jnp.concatenate([block] * terms, axis=1), x)
        halves.append(half.astype(BF16) * flags(s, k))
    return halves


def in_rows(ref):
    return lambda s, k: ref[s, pl.ds(k, 1), :].astype(BF16)


def closed(halves, right, s):
    return dot(jnp.concatenate(halves, axis=1), right[:, s].reshape(-1, right.shape[3]))


def two_terms(x):
    high = x.astype(BF16)
    return jnp.concatenate([high, (x - high.astype(F32)).astype(BF16)], axis=0)


def other_kernel(
    pattern_hbm, left_hbm, right_hbm, guess_hbm, precond_hbm, columns_hbm,
    part, left, right, guess, precond, columns, flags,
    pattern, pattern_sem, columns_sem, guess_sem, left_sem, right_sem, precond_sem,
):
    mine = lax.axis_index("core")
    other = 1 - mine
    small = [
        pltpu.make_async_copy(pattern_hbm, pattern, pattern_sem),
        pltpu.make_async_copy(columns_hbm, columns, columns_sem),
    ]
    copies = []
    for i, s in enumerate((other, mine)):
        copies.append(
            [
                pltpu.make_async_copy(guess_hbm.at[s], guess.at[s], guess_sem.at[i]),
                pltpu.make_async_copy(left_hbm.at[:, s], left.at[:, s], left_sem.at[i]),
                pltpu.make_async_copy(right_hbm.at[:, s], right.at[:, s], right_sem.at[i]),
            ]
        )
    last = pltpu.make_async_copy(precond_hbm, precond, precond_sem)
    for copy in small + copies[0] + copies[1] + [last]:
        copy.start()
    for copy in small:
        copy.wait()
    for s in range(left.shape[1]):
        for k in range(left.shape[0]):
            flags[s, pl.ds(k, 1), :] = jnp.full((1, flags.shape[2]), pattern[s, k].astype(F32))
    copies[0][0].wait()
    copies[0][1].wait()
    halves = halves_of(left, other, in_rows(flags), two_terms(guess[other]))
    copies[0][2].wait()
    turned = columns[other].astype(F32)
    rest = part.shape[0] - right.shape[2] - turned.shape[0]
    rest = jnp.zeros((rest, turned.shape[1]), F32)
    part[...] = jnp.concatenate([closed(halves, right, other), turned, rest], axis=0).astype(BF16)
    for copy in copies[1] + [last]:
        copy.wait()


def own_kernel(flags, left, right, guess, precond, part, level, rows_out, state_rows):
    mine, chip = lax.axis_index("core"), lax.axis_index("chip")
    part[...] = closed(halves_of(left, mine, in_rows(flags), two_terms(guess[mine])), right, mine)
    level[...] = guess[...] / precond[...]
    count = rows_out.shape[1]
    own = pl.ds(pl.multiple_of(chip * count, count), count)
    for i, ref in enumerate((guess, level, precond)):
        rows_out[i] = ref[mine, own, :]
    count = state_rows.shape[2]
    own = pl.ds(pl.multiple_of((chip * 2 + mine) * count, count), count)
    for i, ref in enumerate((guess, level)):
        for s in range(ref.shape[0]):
            state_rows[i, s] = ref[s, own, :]


def chunks_kernel(own, theirs, columns, chunks):
    mine = lax.axis_index("core")
    chips, count, states = chunks.shape
    theirs = theirs[...].astype(F32)
    total = own[...] + theirs[:states]
    a, b = columns[mine].astype(F32), theirs[states : states + columns.shape[1]]
    first = mine == 0
    turned = jnp.concatenate([jnp.where(first, a, b), jnp.where(first, b, a)], axis=0)
    turned = jnp.broadcast_to(turned[None], (chips,) + turned.shape)
    chunks[...] = jnp.concatenate([total.reshape(chips, -1, states), turned], axis=1).astype(BF16)


def rows_kernel(received, rows_in, packed, sums, chunks):
    g, d, p = rows_in[0], rows_in[1], rows_in[2]
    count, states = g.shape
    h = jnp.sum(received[:, :count, :].astype(F32), axis=0)
    y = h / p
    high = y.astype(BF16).astype(F32)
    middle = (y - high).astype(BF16).astype(F32)
    packed[:states, :] = received[:, count:, :].reshape(states, states)
    packed[states:, :] = jnp.concatenate([high, middle, y - high - middle], axis=0).astype(BF16)
    chunks[...] = jnp.broadcast_to(y[None].astype(BF16), chunks.shape)
    pairs = ((g, g), (g, h), (g, d), (d, d), (g, y), (d, y), (y, y), (h, y))
    sums[...] = jnp.concatenate([jnp.sum(a * b, axis=0, keepdims=True) for a, b in pairs], axis=0)


def renorm_kernel(flags, left, right, level, mine, theirs, out, d_hd, state_y):
    first = lax.axis_index("core") == 0
    states = left.shape[2]
    a, b = mine[...].astype(F32), theirs[...].astype(F32)
    count = state_y.shape[1]
    y = []
    for x in (a, b):
        terms = [x[i : i + count] for i in range(states, x.shape[0], count)]
        terms = terms[0::2], terms[1::2]
        low, high = [c[0] + c[1] + c[2] for c in terms]
        y.append(jnp.where(first, low, high))
    a, b = a[:states], b[:states]
    dots = []
    for s in range(left.shape[1]):
        is_mine = first if s == 0 else jnp.logical_not(first)
        state_y[s] = jnp.where(is_mine, y[0], y[1])
        turned = jnp.where(is_mine, a, b)
        rotation = jnp.transpose(turned).astype(BF16)
        turned = turned.astype(BF16)
        for k in range(left.shape[0]):
            rotated = dot(left[k, s], rotation).astype(BF16)
            out[k, s] = dot(turned, rotated).astype(BF16)
        d = level[s]
        image = closed(halves_of(left, s, in_rows(flags), d.astype(BF16)), right, s)
        dots.append(jnp.sum(d * image, axis=0, keepdims=True))
    d_hd[...] = dots[0] + dots[1]


def dots_of(s, flags, y, left, right, level):
    image = closed(halves_of(left, s, in_rows(flags), y), right, s)
    y_hy = jnp.sum(y.astype(F32) * image, axis=0, keepdims=True)
    d_hy = jnp.sum(level[s] * image, axis=0, keepdims=True)
    return jnp.concatenate([y_hy, d_hy], axis=0)


def own_dots_kernel(flags, gathered, left, right, level, d_hd, out):
    y = gathered[...].reshape(left.shape[2:])
    out[...] = jnp.concatenate([dots_of(lax.axis_index("core"), flags, y, left, right, level), d_hd[...]], axis=0)


def other_dots_kernel(flags, gathered, left, right, level, own_dots, row_sums, out):
    y = gathered[...].reshape(left.shape[2:])
    dots = dots_of(1 - lax.axis_index("core"), flags, y, left, right, level)
    sums = jnp.concatenate([row_sums[...], own_dots[...], dots, jnp.zeros((3, y.shape[1]), F32)], axis=0)
    sums = jnp.sum(sums, axis=1, keepdims=True)
    extent = (sums.shape[0], out.shape[2])
    here = lax.broadcasted_iota(jnp.int32, extent, 0) == lax.broadcasted_iota(jnp.int32, extent, 1)
    line = jnp.sum(jnp.where(here, sums, 0.0), axis=0, keepdims=True)
    out[...] = jnp.broadcast_to(line[None], out.shape)


def gather_kernel(received, out):
    out[...] = jnp.broadcast_to(jnp.sum(received[...], axis=0)[None], out.shape)


def state_kernel(entries, received, state_rows, state_y, state, energy_out):
    sums = jnp.sum(received[...], axis=0)
    lanes = [sums[:, i : i + 1] for i in range(13)]
    gg, gh, gd, dd, gy, dy, yy, hy = lanes[:8]
    y_hy, d_hy, d_hd = lanes[8] + lanes[11], lanes[9] + lanes[12], lanes[10]
    inverse = 1.0 / entries
    first_square = 1.0 / (gg * inverse + 1e-06)
    rho = first_square * gh * inverse
    kappa = first_square * (gy - rho * gd) * inverse
    qq = yy - 2.0 * rho * dy + rho * rho * dd - 2.0 * kappa * (gy - rho * gd) + kappa * kappa * gg
    hq = hy - rho * gy - kappa * gh
    q_hq = y_hy - 2.0 * rho * d_hy + rho * rho * d_hd - 2.0 * kappa * (hy - rho * gy) + kappa * kappa * gh
    second_square = 1.0 / (first_square * qq * inverse + 1e-06)
    second_scale = jnp.sqrt(second_square)
    first_scale = jnp.sqrt(first_square)
    coupling = second_scale * first_square * hq * inverse
    rho_second = second_square * first_square * q_hq * inverse
    half_gap = (rho - rho_second) * 0.5
    energy = (rho + rho_second) * 0.5 - jnp.sqrt(half_gap * half_gap + coupling * coupling)
    weight_first = rho_second - energy
    weight_second = -coupling
    scaling = 1.0 / jnp.sqrt(weight_first * weight_first + weight_second * weight_second)
    on_second = weight_second * second_scale * scaling * first_scale
    on_first = weight_first * scaling * first_scale
    energy_out[...] = jnp.broadcast_to(energy, energy_out.shape)
    g, d, y = state_rows[0], state_rows[1], state_y[...]
    state[...] = on_first[None] * g + on_second[None] * (y - rho[None] * d - kappa[None] * g)


def call(kernel, out_shape, in_specs, flops=0, scratch=(), limit=16):
    return pl.pallas_call(
        kernel,
        out_shape=out_shape,
        in_specs=in_specs,
        out_specs=jax.tree.map(lambda _: VMEM, out_shape),
        scratch_shapes=scratch,
        cost_estimate=pl.CostEstimate(flops=flops, bytes_accessed=1 << 20, transcendentals=0),
        compiler_params=pltpu.CompilerParams(vmem_limit_bytes=limit << 20),
    )


def local(left_hbm, right_hbm, pattern, guess_hbm, precond_hbm, rotation):
    ops, sectors, states = left_hbm.shape[:3]
    chips, cores, zones = (lax.axis_size(axis) for axis in ("chip", "core", "sec"))
    count = states // chips
    entries = float(sectors * zones * states * states)
    shape = jax.ShapeDtypeStruct
    dma = pltpu.SemaphoreType.DMA
    block = (states, states)
    flops = 4 * ops * sectors * states**3
    pattern = jnp.swapaxes(pattern, 0, 1)
    columns = jnp.swapaxes(rotation, 1, 2)

    def in_hbm(x):
        return pltpu.with_memory_space_constraint(x, pltpu.HBM)

    def swapped(x):
        return lax.ppermute(x, "core", SWAP)

    part, left, right, guess, precond, columns, flags = call(
        other_kernel,
        (
            shape((states + 16, states), BF16),
            shape(left_hbm.shape, BF16),
            shape(right_hbm.shape, BF16),
            shape(guess_hbm.shape, F32),
            shape(guess_hbm.shape, F32),
            shape(columns.shape, BF16),
            shape((sectors, ops, states), F32),
        ),
        [HBM] * 6,
        flops // 2,
        [pltpu.SMEM(pattern.shape, jnp.int32), dma, dma, dma((2,)), dma((2,)), dma((2,)), dma],
    )(*(in_hbm(x) for x in (pattern, left_hbm, right_hbm, guess_hbm, precond_hbm, columns)))
    theirs = swapped(part)
    own, level, own_rows, state_rows = call(
        own_kernel,
        (
            shape(block, F32),
            shape(guess.shape, F32),
            shape((3, count, states), F32),
            shape((2, sectors, count // cores, states), F32),
        ),
        [VMEM] * 5,
        flops // 2,
    )(flags, left, right, guess, precond)
    chunks = call(chunks_kernel, shape((chips, 2 * count, states), BF16), [VMEM] * 3)(own, theirs, columns)
    received = lax.all_to_all(chunks, "chip", 0, 0)
    packed, row_sums, chunks = call(
        rows_kernel,
        (shape((states + 3 * count, states), BF16), shape((8, states), F32), shape((chips, count, states), BF16)),
        [VMEM] * 2,
    )(received, own_rows)
    gathered = lax.all_to_all(chunks, "chip", 0, 0)
    renormalized, d_hd, state_y = call(
        renorm_kernel,
        (shape(left.shape, BF16), shape((1, states), F32), shape((sectors, count // cores, states), F32)),
        [VMEM] * 6,
        2 * flops,
    )(flags, left, right, level, packed, swapped(packed))
    gathered, d_hd = lax.optimization_barrier((gathered, d_hd))
    gathered_theirs = swapped(gathered)
    dots = call(own_dots_kernel, shape((3, states), F32), [VMEM] * 6, flops // 2)(
        flags, gathered, left, right, level, d_hd
    )
    sums = call(other_dots_kernel, shape((chips, 1, 128), F32), [VMEM] * 7, flops // 2)(
        flags, gathered_theirs, left, right, level, dots, row_sums
    )
    sums = lax.all_to_all(sums, "chip", 0, 0)
    sums = call(gather_kernel, shape((cores * zones, 1, 128), F32), [VMEM])(sums)
    sums = lax.all_to_all(sums, ("core", "sec"), 0, 0)
    new_state, energy = call(
        lambda *refs: state_kernel(entries, *refs),
        (shape((sectors, count // cores, states), F32), shape((1, 128), F32)),
        [VMEM] * 3,
    )(sums, state_rows, state_y)
    return new_state, energy[0, :1], renormalized


def solution(mesh):
    cores = 2
    mesh = Mesh(mesh.devices.reshape(-1, cores, mesh.shape["sec"]), ("chip", "core", "sec"))
    return jax.shard_map(
        local,
        mesh=mesh,
        in_specs=(
            P(OPS, "sec", None, None),
            P(OPS, "sec", None, None),
            P(OPS, "sec"),
            P("sec", None, None),
            P("sec", None, None),
            P("sec", None, OPS),
        ),
        out_specs=(P("sec", OPS, None), P(), P(OPS, "sec", None, None)),
        check_vma=False,
    )
```

```python
import jax
import jax.numpy as jnp
from jax import lax
from jax.experimental import pallas as pl
from jax.experimental.pallas import tpu as pltpu
from jax.sharding import Mesh, PartitionSpec as P

F32 = jnp.float32
BF16 = jnp.bfloat16
OPS = ("chip", "core")
SWAP = [(0, 1), (1, 0)]
VMEM = pl.BlockSpec(memory_space=pltpu.VMEM)
SMEM = pl.BlockSpec(memory_space=pltpu.SMEM)
HBM = pl.BlockSpec(memory_space=pltpu.HBM)


def dot(a, b):
    return jnp.dot(a, b, preferred_element_type=F32)


def image_of(x, left, right, flags):
    count, states = left.shape[:2]
    terms = x.shape[0] // states
    halves = []
    for k in range(count):
        block = left[k]
        half = dot(jnp.concatenate([block] * terms, axis=1), x).astype(BF16)
        halves.append(half * flags[k : k + 1, :].astype(BF16))
    return dot(jnp.concatenate(halves, axis=1), right[...].reshape(count * states, states))


def chip_image(x, flags, left, right, left_swapped, right_swapped):
    count = left.shape[0]
    own = image_of(x, left, right, flags.at[pl.ds(0, count)])
    return own + image_of(x, left_swapped, right_swapped, flags.at[pl.ds(count, count)])


def two_terms(x):
    high = x.astype(BF16)
    return jnp.concatenate([high, (x - high.astype(F32)).astype(BF16)], axis=0)


def other_kernel(
    pattern_hbm, left_hbm, right_hbm, guess_hbm, precond_hbm, columns_hbm,
    part, left, left_other, right, right_other, guess, precond, rows_other, columns, flags,
    pattern, pattern_sem, columns_sem, rows_sem, guess_sem, left_sem, right_sem, precond_sem,
):
    mine, chip = lax.axis_index("core"), lax.axis_index("chip")
    other = 1 - mine
    count = rows_other.shape[0]
    own = pl.ds(pl.multiple_of((chip * 2 + mine) * count, count), count)
    small = [
        pltpu.make_async_copy(pattern_hbm, pattern, pattern_sem),
        pltpu.make_async_copy(columns_hbm, columns, columns_sem),
    ]
    copies = []
    for i, (s, l, r) in enumerate(((other, left_other, right_other), (mine, left, right))):
        copies.append(
            [
                pltpu.make_async_copy(guess_hbm.at[s], guess.at[s], guess_sem.at[i]),
                pltpu.make_async_copy(left_hbm.at[:, s], l, left_sem.at[i]),
                pltpu.make_async_copy(right_hbm.at[:, s], r, right_sem.at[i]),
            ]
        )
    last = [
        pltpu.make_async_copy(precond_hbm.at[mine], precond, precond_sem),
        pltpu.make_async_copy(precond_hbm.at[other, own], rows_other, rows_sem),
    ]
    for copy in small + copies[0] + copies[1] + last:
        copy.start()
    for copy in small:
        copy.wait()
    for s in range(flags.shape[0]):
        for k in range(flags.shape[1]):
            flags[s, pl.ds(k, 1), :] = jnp.full((1, flags.shape[2]), pattern[s, k].astype(F32))
    turned = columns[other].astype(F32)
    ones = flags[other]
    rest = jnp.zeros((part.shape[0] - guess.shape[1] - turned.shape[0] - ones.shape[0], turned.shape[1]), F32)
    for copy in copies[0]:
        copy.wait()
    image = image_of(two_terms(guess[other]), left_other, right_other, flags.at[other])
    part[...] = jnp.concatenate([image, turned, ones, rest], axis=0).astype(BF16)
    for copy in copies[1] + last:
        copy.wait()


def own_kernel(flags, left, right, guess, precond, rows_other, part, level, rows_out, state_rows):
    mine, chip = lax.axis_index("core"), lax.axis_index("chip")
    other = 1 - mine
    part[...] = image_of(two_terms(guess[mine]), left, right, flags.at[mine])
    level[...] = guess[mine] / precond[...]
    count = rows_out.shape[1]
    own = pl.ds(pl.multiple_of(chip * count, count), count)
    rows_out[0] = guess[mine, own, :]
    rows_out[1] = level[own, :]
    rows_out[2] = precond[own, :]
    count = state_rows.shape[2]
    own = pl.ds(pl.multiple_of((chip * 2 + mine) * count, count), count)
    state_rows[0, mine] = guess[mine, own, :]
    state_rows[1, mine] = level[own, :]
    state_rows[0, other] = guess[other, own, :]
    state_rows[1, other] = guess[other, own, :] / rows_other[...]


def chunks_kernel(own, theirs, columns, flags, chunks, all_flags):
    mine = lax.axis_index("core")
    chips, count, states = chunks.shape
    theirs = theirs[...].astype(F32)
    total = own[...] + theirs[:states]
    a, b = columns[mine].astype(F32), theirs[states : states + columns.shape[1]]
    first = mine == 0
    turned = jnp.concatenate([jnp.where(first, a, b), jnp.where(first, b, a)], axis=0)
    turned = jnp.broadcast_to(turned[None], (chips,) + turned.shape)
    ones = theirs[states + columns.shape[1] :][: flags.shape[1]]
    all_flags[...] = jnp.concatenate([flags[mine], ones], axis=0)
    chunks[...] = jnp.concatenate([total.reshape(chips, -1, states), turned], axis=1).astype(BF16)


def rows_kernel(received, rows_in, packed, sums, chunks):
    g, d, p = rows_in[0], rows_in[1], rows_in[2]
    count, states = g.shape
    h = jnp.sum(received[:, :count, :].astype(F32), axis=0)
    y = h / p
    high = y.astype(BF16).astype(F32)
    middle = (y - high).astype(BF16).astype(F32)
    packed[:states, :] = received[:, count:, :].reshape(states, states)
    packed[states:, :] = jnp.concatenate([high, middle, y - high - middle], axis=0).astype(BF16)
    chunks[...] = jnp.broadcast_to(y[None].astype(BF16), chunks.shape)
    pairs = ((g, g), (g, h), (g, d), (d, d), (g, y), (d, y), (y, y), (h, y))
    sums[...] = jnp.concatenate([jnp.sum(a * b, axis=0, keepdims=True) for a, b in pairs], axis=0)


def renorm_kernel(flags, left, left_other, right, left_swapped, right_swapped, level, packed, packed_theirs, out, d_hd, state_y):
    mine = lax.axis_index("core")
    first = mine == 0
    states = left.shape[2]
    a, b = packed[...].astype(F32), packed_theirs[...].astype(F32)
    count = state_y.shape[1]
    y = []
    for x in (a, b):
        terms = [x[i : i + count] for i in range(states, x.shape[0], count)]
        terms = terms[0::2], terms[1::2]
        low, high = [c[0] + c[1] + c[2] for c in terms]
        y.append(jnp.where(first, low, high))
    state_y[mine] = y[0]
    state_y[1 - mine] = y[1]
    for s, turned, blocks in ((mine, a[:states], left), (1 - mine, b[:states], left_other)):
        rotation = jnp.transpose(turned).astype(BF16)
        turned = turned.astype(BF16)
        for k in range(blocks.shape[0]):
            rotated = dot(blocks[k], rotation).astype(BF16)
            out[k, s] = dot(turned, rotated).astype(BF16)
    low = level[...].astype(BF16)
    image = chip_image(low, flags, left, right, left_swapped, right_swapped)
    d_hd[...] = jnp.sum(level[...] * image, axis=0, keepdims=True)


def dots_kernel(flags, gathered, left, right, left_swapped, right_swapped, level, row_sums, d_hd, out):
    y = gathered[...].reshape(level.shape)
    image = chip_image(y, flags, left, right, left_swapped, right_swapped)
    y_hy = jnp.sum(y.astype(F32) * image, axis=0, keepdims=True)
    d_hy = jnp.sum(level[...] * image, axis=0, keepdims=True)
    rest = jnp.zeros((5, y.shape[1]), F32)
    sums = jnp.concatenate([row_sums[...], y_hy, d_hy, d_hd[...], rest], axis=0)
    sums = jnp.sum(sums, axis=1, keepdims=True)
    extent = (sums.shape[0], out.shape[2])
    here = lax.broadcasted_iota(jnp.int32, extent, 0) == lax.broadcasted_iota(jnp.int32, extent, 1)
    line = jnp.sum(jnp.where(here, sums, 0.0), axis=0, keepdims=True)
    out[...] = jnp.broadcast_to(line[None], out.shape)


def gather_kernel(received, out):
    out[...] = jnp.broadcast_to(jnp.sum(received[...], axis=0)[None], out.shape)


def state_kernel(entries, received, state_rows, state_y, state, energy_out):
    sums = jnp.sum(received[...], axis=0)
    extent = (16, sums.shape[1])
    here = lax.broadcasted_iota(jnp.int32, extent, 0) == lax.broadcasted_iota(jnp.int32, extent, 1)
    sums = jnp.sum(jnp.where(here, jnp.broadcast_to(sums, extent), 0.0), axis=1, keepdims=True)
    sums = jnp.broadcast_to(sums, (extent[0], state.shape[2]))
    gg, gh, gd, dd, gy, dy, yy, hy, y_hy, d_hy, d_hd = [sums[i : i + 1] for i in range(11)]
    inverse = 1.0 / entries
    first_square = 1.0 / (gg * inverse + 1e-06)
    rho = first_square * gh * inverse
    kappa = first_square * (gy - rho * gd) * inverse
    qq = yy - 2.0 * rho * dy + rho * rho * dd - 2.0 * kappa * (gy - rho * gd) + kappa * kappa * gg
    hq = hy - rho * gy - kappa * gh
    q_hq = y_hy - 2.0 * rho * d_hy + rho * rho * d_hd - 2.0 * kappa * (hy - rho * gy) + kappa * kappa * gh
    second_square = 1.0 / (first_square * qq * inverse + 1e-06)
    second_scale = jnp.sqrt(second_square)
    first_scale = jnp.sqrt(first_square)
    coupling = second_scale * first_square * hq * inverse
    rho_second = second_square * first_square * q_hq * inverse
    half_gap = (rho - rho_second) * 0.5
    energy = (rho + rho_second) * 0.5 - jnp.sqrt(half_gap * half_gap + coupling * coupling)
    weight_first = rho_second - energy
    weight_second = -coupling
    scaling = 1.0 / jnp.sqrt(weight_first * weight_first + weight_second * weight_second)
    on_second = weight_second * second_scale * scaling * first_scale
    on_first = weight_first * scaling * first_scale
    energy_out[...] = energy[:, : energy_out.shape[1]]
    g, d, y = state_rows[0], state_rows[1], state_y[...]
    state[...] = on_first[None] * g + on_second[None] * (y - rho[None] * d - kappa[None] * g)


def call(kernel, out_shape, in_specs, flops=0, scratch=(), limit=16):
    return pl.pallas_call(
        kernel,
        out_shape=out_shape,
        in_specs=in_specs,
        out_specs=jax.tree.map(lambda _: VMEM, out_shape),
        scratch_shapes=scratch,
        cost_estimate=pl.CostEstimate(flops=flops, bytes_accessed=1 << 20, transcendentals=0),
        compiler_params=pltpu.CompilerParams(vmem_limit_bytes=limit << 20),
    )


def local(left_hbm, right_hbm, pattern, guess_hbm, precond_hbm, rotation):
    ops, sectors, states = left_hbm.shape[:3]
    chips, cores, zones = (lax.axis_size(axis) for axis in ("chip", "core", "sec"))
    count = states // chips
    entries = float(sectors * zones * states * states)
    shape = jax.ShapeDtypeStruct
    dma = pltpu.SemaphoreType.DMA
    block = (states, states)
    flops = 4 * ops * sectors * states**3
    pattern = jnp.swapaxes(pattern, 0, 1)
    columns = jnp.swapaxes(rotation, 1, 2)

    def in_hbm(x):
        return pltpu.with_memory_space_constraint(x, pltpu.HBM)

    def swap(x):
        return lax.ppermute(x, "core", SWAP)

    operators = shape((ops,) + block, BF16)
    part, left, left_other, right, right_other, guess, precond, rows_other, columns, flags = call(
        other_kernel,
        (
            shape((states + 16, states), BF16),
            operators,
            operators,
            operators,
            operators,
            shape(guess_hbm.shape, F32),
            shape(block, F32),
            shape((count // cores, states), F32),
            shape(columns.shape, BF16),
            shape((sectors, ops, states), F32),
        ),
        [HBM] * 6,
        flops // 2,
        [pltpu.SMEM(pattern.shape, jnp.int32), dma, dma, dma, dma((2,)), dma((2,)), dma((2,)), dma],
    )(*(in_hbm(x) for x in (pattern, left_hbm, right_hbm, guess_hbm, precond_hbm, columns)))
    theirs = swap(part)
    own, level, own_rows, state_rows = call(
        own_kernel,
        (
            shape(block, F32),
            shape(block, F32),
            shape((3, count, states), F32),
            shape((2, sectors, count // cores, states), F32),
        ),
        [VMEM] * 6,
        flops // 2,
    )(flags, left, right, guess, precond, rows_other)
    chunks, flags = call(
        chunks_kernel,
        (shape((chips, 2 * count, states), BF16), shape((2 * ops, states), F32)),
        [VMEM] * 4,
    )(own, theirs, columns, flags)
    chunks, left_other, right_other = lax.optimization_barrier((chunks, left_other, right_other))
    left_swapped, right_swapped = swap(left_other), swap(right_other)
    received = lax.all_to_all(chunks, "chip", 0, 0)
    received, left_swapped, right_swapped = lax.optimization_barrier((received, left_swapped, right_swapped))
    packed, row_sums, chunks = call(
        rows_kernel,
        (shape((states + 3 * count, states), BF16), shape((8, states), F32), shape((chips, count, states), BF16)),
        [VMEM] * 2,
    )(received, own_rows)
    gathered = lax.all_to_all(chunks, "chip", 0, 0)
    renormalized, d_hd, state_y = call(
        renorm_kernel,
        (shape(left_hbm.shape, BF16), shape((1, states), F32), shape((sectors, count // cores, states), F32)),
        [VMEM] * 9,
        2 * flops,
    )(flags, left, left_other, right, left_swapped, right_swapped, level, packed, swap(packed))
    gathered, d_hd = lax.optimization_barrier((gathered, d_hd))
    sums = call(dots_kernel, shape((chips, 1, 128), F32), [VMEM] * 9, flops)(
        flags, gathered, left, right, left_swapped, right_swapped, level, row_sums, d_hd
    )
    sums = lax.all_to_all(sums, "chip", 0, 0)
    sums = call(gather_kernel, shape((cores * zones, 1, 128), F32), [VMEM])(sums)
    sums = lax.all_to_all(sums, ("core", "sec"), 0, 0)
    new_state, energy = call(
        lambda *refs: state_kernel(entries, *refs),
        (shape((sectors, count // cores, states), F32), shape((1, 128), F32)),
        [VMEM] * 3,
    )(sums, state_rows, state_y)
    return new_state, energy[0, :1], renormalized


def solution(mesh):
    cores = 2
    mesh = Mesh(mesh.devices.reshape(-1, cores, mesh.shape["sec"]), ("chip", "core", "sec"))
    return jax.shard_map(
        local,
        mesh=mesh,
        in_specs=(
            P(OPS, "sec", None, None),
            P(OPS, "sec", None, None),
            P(OPS, "sec"),
            P("sec", None, None),
            P("sec", None, None),
            P("sec", None, OPS),
        ),
        out_specs=(P("sec", OPS, None), P(), P(OPS, "sec", None, None)),
        check_vma=False,
    )
```

```python
import jax
import jax.numpy as jnp
from jax import lax
from jax.experimental import pallas as pl
from jax.experimental.pallas import tpu as pltpu
from jax.sharding import Mesh, PartitionSpec as P

F32 = jnp.float32
BF16 = jnp.bfloat16
OPS = ("chip", "core")
SWAP = [(0, 1), (1, 0)]
VMEM = pl.BlockSpec(memory_space=pltpu.VMEM)
SMEM = pl.BlockSpec(memory_space=pltpu.SMEM)
HBM = pl.BlockSpec(memory_space=pltpu.HBM)


def dot(a, b):
    return jnp.dot(a, b, preferred_element_type=F32)


def image_of(x, left, right, flags):
    count, states = left.shape[:2]
    terms = x.shape[0] // states
    halves = []
    for k in range(count):
        block = left[k]
        half = dot(jnp.concatenate([block] * terms, axis=1), x).astype(BF16)
        parts = [half[:, i : i + states] for i in range(0, half.shape[1], states)]
        halves.append(jnp.concatenate(parts, axis=0) * flags[k : k + 1, :].astype(BF16))
    return dot(jnp.concatenate(halves, axis=1), right[...].reshape(count * states, states))


def chip_image(x, flags, left, right, swapped):
    count = left.shape[0]
    own = image_of(x, left, right, flags.at[pl.ds(0, count)])
    return own + image_of(x, swapped.at[0], swapped.at[1], flags.at[pl.ds(count, count)])


def two_terms(x):
    high = x.astype(BF16)
    return jnp.concatenate([high, (x - high.astype(F32)).astype(BF16)], axis=0)


def other_kernel(
    pattern_hbm, left_hbm, right_hbm, guess_hbm, precond_hbm, columns_hbm,
    part, left, right, operators, guess, precond, rows_other, columns, flags,
    pattern, pattern_sem, columns_sem, rows_sem, guess_sem, left_sem, right_sem, precond_sem,
):
    mine, chip = lax.axis_index("core"), lax.axis_index("chip")
    other = 1 - mine
    count = rows_other.shape[0]
    own = pl.ds(pl.multiple_of((chip * 2 + mine) * count, count), count)
    small = [
        pltpu.make_async_copy(pattern_hbm, pattern, pattern_sem),
        pltpu.make_async_copy(columns_hbm, columns, columns_sem),
    ]
    copies = []
    for i, (s, l, r) in enumerate(((other, operators.at[0], operators.at[1]), (mine, left, right))):
        copies.append(
            [
                pltpu.make_async_copy(guess_hbm.at[s], guess.at[s], guess_sem.at[i]),
                pltpu.make_async_copy(left_hbm.at[:, s], l, left_sem.at[i]),
                pltpu.make_async_copy(right_hbm.at[:, s], r, right_sem.at[i]),
            ]
        )
    last = [
        pltpu.make_async_copy(precond_hbm.at[mine], precond, precond_sem),
        pltpu.make_async_copy(precond_hbm.at[other, own], rows_other, rows_sem),
    ]
    for copy in small + copies[0] + copies[1] + last:
        copy.start()
    for copy in small:
        copy.wait()
    for s in range(flags.shape[0]):
        for k in range(flags.shape[1]):
            flags[s, pl.ds(k, 1), :] = jnp.full((1, flags.shape[2]), pattern[s, k].astype(F32))
    turned = columns[other].astype(F32)
    ones = flags[other]
    rest = jnp.zeros((part.shape[0] - guess.shape[1] - turned.shape[0] - ones.shape[0], turned.shape[1]), F32)
    for copy in copies[0]:
        copy.wait()
    image = image_of(two_terms(guess[other]), operators.at[0], operators.at[1], flags.at[other])
    part[...] = jnp.concatenate([image, turned, ones, rest], axis=0).astype(BF16)
    for copy in copies[1] + last:
        copy.wait()


def own_kernel(flags, left, right, guess, precond, rows_other, part, level, rows_out, state_rows):
    mine, chip = lax.axis_index("core"), lax.axis_index("chip")
    other = 1 - mine
    part[...] = image_of(two_terms(guess[mine]), left, right, flags.at[mine])
    level[...] = guess[mine] / precond[...]
    count = rows_out.shape[1]
    own = pl.ds(pl.multiple_of(chip * count, count), count)
    rows_out[0] = guess[mine, own, :]
    rows_out[1] = level[own, :]
    rows_out[2] = precond[own, :]
    count = state_rows.shape[2]
    own = pl.ds(pl.multiple_of((chip * 2 + mine) * count, count), count)
    state_rows[0, mine] = guess[mine, own, :]
    state_rows[1, mine] = level[own, :]
    state_rows[0, other] = guess[other, own, :]
    state_rows[1, other] = guess[other, own, :] / rows_other[...]


def chunks_kernel(own, theirs, columns, flags, chunks, all_flags):
    mine = lax.axis_index("core")
    chips, count, states = chunks.shape
    theirs = theirs[...].astype(F32)
    total = own[...] + theirs[:states]
    a, b = columns[mine].astype(F32), theirs[states : states + columns.shape[1]]
    first = mine == 0
    turned = jnp.concatenate([jnp.where(first, a, b), jnp.where(first, b, a)], axis=0)
    turned = jnp.broadcast_to(turned[None], (chips,) + turned.shape)
    ones = theirs[states + columns.shape[1] :][: flags.shape[1]]
    all_flags[...] = jnp.concatenate([flags[mine], ones], axis=0)
    chunks[...] = jnp.concatenate([total.reshape(chips, -1, states), turned], axis=1).astype(BF16)


def rows_kernel(received, rows_in, packed, sums, chunks):
    g, d, p = rows_in[0], rows_in[1], rows_in[2]
    count, states = g.shape
    h = jnp.sum(received[:, :count, :].astype(F32), axis=0)
    y = h / p
    high = y.astype(BF16).astype(F32)
    middle = (y - high).astype(BF16).astype(F32)
    packed[:states, :] = received[:, count:, :].reshape(states, states)
    packed[states:, :] = jnp.concatenate([high, middle, y - high - middle], axis=0).astype(BF16)
    chunks[...] = jnp.broadcast_to(y[None].astype(BF16), chunks.shape)
    pairs = ((g, g), (g, h), (g, d), (d, d), (g, y), (d, y), (y, y), (h, y))
    sums[...] = jnp.concatenate([jnp.sum(a * b, axis=0, keepdims=True) for a, b in pairs], axis=0)


def renorm_kernel(left, operators, packed, packed_theirs, out, state_y):
    mine = lax.axis_index("core")
    first = mine == 0
    states = left.shape[2]
    a, b = packed[...].astype(F32), packed_theirs[...].astype(F32)
    count = state_y.shape[1]
    y = []
    for x in (a, b):
        terms = [x[i : i + count] for i in range(states, x.shape[0], count)]
        terms = terms[0::2], terms[1::2]
        low, high = [c[0] + c[1] + c[2] for c in terms]
        y.append(jnp.where(first, low, high))
    state_y[mine] = y[0]
    state_y[1 - mine] = y[1]
    for s, turned, blocks in ((mine, a[:states], left), (1 - mine, b[:states], operators.at[0])):
        rotation = jnp.transpose(turned).astype(BF16)
        turned = turned.astype(BF16)
        for k in range(blocks.shape[0]):
            rotated = dot(blocks[k], rotation).astype(BF16)
            out[k, s] = dot(turned, rotated).astype(BF16)


def dots_kernel(flags, gathered, left, right, swapped, level, row_sums, out):
    y = gathered[...].reshape(level.shape)
    states = y.shape[1]
    images = chip_image(jnp.concatenate([y, level[...].astype(BF16)], axis=1), flags, left, right, swapped)
    image = images[:states]
    d_hd = jnp.sum(level[...] * images[states:], axis=0, keepdims=True)
    y_hy = jnp.sum(y.astype(F32) * image, axis=0, keepdims=True)
    d_hy = jnp.sum(level[...] * image, axis=0, keepdims=True)
    rest = jnp.zeros((5, y.shape[1]), F32)
    sums = jnp.concatenate([row_sums[...], y_hy, d_hy, d_hd, rest], axis=0)
    sums = jnp.sum(sums, axis=1, keepdims=True)
    extent = (sums.shape[0], out.shape[1])
    here = lax.broadcasted_iota(jnp.int32, extent, 0) == lax.broadcasted_iota(jnp.int32, extent, 1)
    line = jnp.sum(jnp.where(here, sums, 0.0), axis=0, keepdims=True)
    out[...] = jnp.broadcast_to(line, out.shape)


def state_kernel(entries, received, state_rows, state_y, state, energy_out):
    sums = jnp.sum(received[...], axis=0, keepdims=True)
    extent = (16, sums.shape[1])
    here = lax.broadcasted_iota(jnp.int32, extent, 0) == lax.broadcasted_iota(jnp.int32, extent, 1)
    sums = jnp.sum(jnp.where(here, jnp.broadcast_to(sums, extent), 0.0), axis=1, keepdims=True)
    sums = jnp.broadcast_to(sums, (extent[0], state.shape[2]))
    gg, gh, gd, dd, gy, dy, yy, hy, y_hy, d_hy, d_hd = [sums[i : i + 1] for i in range(11)]
    inverse = 1.0 / entries
    first_square = 1.0 / (gg * inverse + 1e-06)
    rho = first_square * gh * inverse
    kappa = first_square * (gy - rho * gd) * inverse
    qq = yy - 2.0 * rho * dy + rho * rho * dd - 2.0 * kappa * (gy - rho * gd) + kappa * kappa * gg
    hq = hy - rho * gy - kappa * gh
    q_hq = y_hy - 2.0 * rho * d_hy + rho * rho * d_hd - 2.0 * kappa * (hy - rho * gy) + kappa * kappa * gh
    second_square = 1.0 / (first_square * qq * inverse + 1e-06)
    second_scale = jnp.sqrt(second_square)
    first_scale = jnp.sqrt(first_square)
    coupling = second_scale * first_square * hq * inverse
    rho_second = second_square * first_square * q_hq * inverse
    half_gap = (rho - rho_second) * 0.5
    energy = (rho + rho_second) * 0.5 - jnp.sqrt(half_gap * half_gap + coupling * coupling)
    weight_first = rho_second - energy
    weight_second = -coupling
    scaling = 1.0 / jnp.sqrt(weight_first * weight_first + weight_second * weight_second)
    on_second = weight_second * second_scale * scaling * first_scale
    on_first = weight_first * scaling * first_scale
    energy_out[...] = energy[:, : energy_out.shape[1]]
    g, d, y = state_rows[0], state_rows[1], state_y[...]
    state[...] = on_first[None] * g + on_second[None] * (y - rho[None] * d - kappa[None] * g)


def call(kernel, out_shape, in_specs, flops=0, scratch=(), limit=16):
    return pl.pallas_call(
        kernel,
        out_shape=out_shape,
        in_specs=in_specs,
        out_specs=jax.tree.map(lambda _: VMEM, out_shape),
        scratch_shapes=scratch,
        cost_estimate=pl.CostEstimate(flops=flops, bytes_accessed=1 << 20, transcendentals=0),
        compiler_params=pltpu.CompilerParams(vmem_limit_bytes=limit << 20),
    )


def local(left_hbm, right_hbm, pattern, guess_hbm, precond_hbm, rotation):
    ops, sectors, states = left_hbm.shape[:3]
    chips, cores, zones = (lax.axis_size(axis) for axis in ("chip", "core", "sec"))
    count = states // chips
    entries = float(sectors * zones * states * states)
    shape = jax.ShapeDtypeStruct
    dma = pltpu.SemaphoreType.DMA
    block = (states, states)
    flops = 4 * ops * sectors * states**3
    pattern = jnp.swapaxes(pattern, 0, 1)
    columns = jnp.swapaxes(rotation, 1, 2)

    def in_hbm(x):
        return pltpu.with_memory_space_constraint(x, pltpu.HBM)

    def swap(x):
        return lax.ppermute(x, "core", SWAP)

    operators = shape((ops,) + block, BF16)
    part, left, right, others, guess, precond, rows_other, columns, flags = call(
        other_kernel,
        (
            shape((states + 16, states), BF16),
            operators,
            operators,
            shape((2, ops) + block, BF16),
            shape(guess_hbm.shape, F32),
            shape(block, F32),
            shape((count // cores, states), F32),
            shape(columns.shape, BF16),
            shape((sectors, ops, states), F32),
        ),
        [HBM] * 6,
        flops // 2,
        [pltpu.SMEM(pattern.shape, jnp.int32), dma, dma, dma, dma((2,)), dma((2,)), dma((2,)), dma],
    )(*(in_hbm(x) for x in (pattern, left_hbm, right_hbm, guess_hbm, precond_hbm, columns)))
    theirs = swap(part)
    own, level, own_rows, state_rows = call(
        own_kernel,
        (
            shape(block, F32),
            shape(block, F32),
            shape((3, count, states), F32),
            shape((2, sectors, count // cores, states), F32),
        ),
        [VMEM] * 6,
        flops // 2,
    )(flags, left, right, guess, precond, rows_other)
    chunks, flags = call(
        chunks_kernel,
        (shape((chips, 2 * count, states), BF16), shape((2 * ops, states), F32)),
        [VMEM] * 4,
    )(own, theirs, columns, flags)
    chunks, others = lax.optimization_barrier((chunks, others))
    swapped = swap(others)
    received = lax.all_to_all(chunks, "chip", 0, 0)
    received, swapped = lax.optimization_barrier((received, swapped))
    packed, row_sums, chunks = call(
        rows_kernel,
        (shape((states + 3 * count, states), BF16), shape((8, states), F32), shape((chips, count, states), BF16)),
        [VMEM] * 2,
    )(received, own_rows)
    gathered = lax.all_to_all(chunks, "chip", 0, 0)
    sums = call(dots_kernel, shape((chips * cores * zones, 128), F32), [VMEM] * 7, flops)(
        flags, gathered, left, right, swapped, level, row_sums
    )
    sums, packed = lax.optimization_barrier((sums, packed))
    sums = lax.all_to_all(sums, OPS + ("sec",), 0, 0)
    renormalized, state_y = call(
        renorm_kernel,
        (shape(left_hbm.shape, BF16), shape((sectors, count // cores, states), F32)),
        [VMEM] * 4,
        2 * flops,
    )(left, others, packed, swap(packed))
    new_state, energy = call(
        lambda *refs: state_kernel(entries, *refs),
        (shape((sectors, count // cores, states), F32), shape((1, 128), F32)),
        [VMEM] * 3,
    )(sums, state_rows, state_y)
    return new_state, energy[0, :1], renormalized


def solution(mesh):
    cores = 2
    mesh = Mesh(mesh.devices.reshape(-1, cores, mesh.shape["sec"]), ("chip", "core", "sec"))
    return jax.shard_map(
        local,
        mesh=mesh,
        in_specs=(
            P(OPS, "sec", None, None),
            P(OPS, "sec", None, None),
            P(OPS, "sec"),
            P("sec", None, None),
            P("sec", None, None),
            P("sec", None, OPS),
        ),
        out_specs=(P("sec", OPS, None), P(), P(OPS, "sec", None, None)),
        check_vma=False,
    )
```

```python
import jax
import jax.numpy as jnp
from jax import lax
from jax.experimental import pallas as pl
from jax.experimental.pallas import tpu as pltpu
from jax.sharding import Mesh, PartitionSpec as P

F32 = jnp.float32
BF16 = jnp.bfloat16
OPS = ("chip", "core")
SWAP = [(0, 1), (1, 0)]
VMEM = pl.BlockSpec(memory_space=pltpu.VMEM)
SMEM = pl.BlockSpec(memory_space=pltpu.SMEM)
HBM = pl.BlockSpec(memory_space=pltpu.HBM)


def dot(a, b):
    return jnp.dot(a, b, preferred_element_type=F32)


def image_of(x, left, right, flags):
    count, states = left.shape[:2]
    terms = x.shape[0] // states
    halves = []
    for k in range(count):
        block = left[k]
        half = dot(jnp.concatenate([block] * terms, axis=1), x).astype(BF16)
        parts = [half[:, i : i + states] for i in range(0, half.shape[1], states)]
        halves.append(jnp.concatenate(parts, axis=0) * flags[k : k + 1, :].astype(BF16))
    return dot(jnp.concatenate(halves, axis=1), right[...].reshape(count * states, states))


def chip_image(x, flags, left, right, swapped):
    count = left.shape[0]
    own = image_of(x, left, right, flags.at[pl.ds(0, count)])
    return own + image_of(x, swapped.at[0], swapped.at[1], flags.at[pl.ds(count, count)])


def two_terms(x):
    high = x.astype(BF16)
    return jnp.concatenate([high, (x - high.astype(F32)).astype(BF16)], axis=0)


def other_kernel(
    pattern_hbm, left_hbm, right_hbm, guess_hbm, precond_hbm, columns_hbm,
    part, left, right, operators, guess, precond, rows_other, columns, flags,
    pattern, pattern_sem, columns_sem, rows_sem, guess_sem, left_sem, right_sem, precond_sem,
):
    mine, chip = lax.axis_index("core"), lax.axis_index("chip")
    other = 1 - mine
    count = rows_other.shape[0]
    own = pl.ds(pl.multiple_of((chip * 2 + mine) * count, count), count)
    small = [
        pltpu.make_async_copy(pattern_hbm, pattern, pattern_sem),
        pltpu.make_async_copy(columns_hbm, columns, columns_sem),
    ]
    copies = []
    for i, (s, l, r) in enumerate(((other, operators.at[0], operators.at[1]), (mine, left, right))):
        copies.append(
            [
                pltpu.make_async_copy(guess_hbm.at[s], guess.at[s], guess_sem.at[i]),
                pltpu.make_async_copy(left_hbm.at[:, s], l, left_sem.at[i]),
                pltpu.make_async_copy(right_hbm.at[:, s], r, right_sem.at[i]),
            ]
        )
    last = [
        pltpu.make_async_copy(precond_hbm.at[mine], precond, precond_sem),
        pltpu.make_async_copy(precond_hbm.at[other, own], rows_other, rows_sem),
    ]
    for copy in small + copies[0] + copies[1] + last:
        copy.start()
    for copy in small:
        copy.wait()
    for s in range(flags.shape[0]):
        for k in range(flags.shape[1]):
            flags[s, pl.ds(k, 1), :] = jnp.full((1, flags.shape[2]), pattern[s, k].astype(F32))
    turned = columns[other].astype(F32)
    ones = flags[other]
    rest = jnp.zeros((part.shape[0] - guess.shape[1] - turned.shape[0] - ones.shape[0], turned.shape[1]), F32)
    for copy in copies[0]:
        copy.wait()
    image = image_of(two_terms(guess[other]), operators.at[0], operators.at[1], flags.at[other])
    part[...] = jnp.concatenate([image, turned, ones, rest], axis=0).astype(BF16)
    for copy in copies[1] + last:
        copy.wait()


def own_kernel(flags, left, right, guess, precond, rows_other, part, level, rows_out, state_rows):
    mine, chip = lax.axis_index("core"), lax.axis_index("chip")
    other = 1 - mine
    part[...] = image_of(two_terms(guess[mine]), left, right, flags.at[mine])
    level[...] = guess[mine] / precond[...]
    count = rows_out.shape[1]
    own = pl.ds(pl.multiple_of(chip * count, count), count)
    rows_out[0] = guess[mine, own, :]
    rows_out[1] = level[own, :]
    rows_out[2] = precond[own, :]
    count = state_rows.shape[2]
    own = pl.ds(pl.multiple_of((chip * 2 + mine) * count, count), count)
    state_rows[0, mine] = guess[mine, own, :]
    state_rows[1, mine] = level[own, :]
    state_rows[0, other] = guess[other, own, :]
    state_rows[1, other] = guess[other, own, :] / rows_other[...]


def chunks_kernel(own, theirs, columns, flags, chunks, all_flags):
    mine = lax.axis_index("core")
    chips, count, states = chunks.shape
    theirs = theirs[...].astype(F32)
    total = own[...] + theirs[:states]
    a, b = columns[mine].astype(F32), theirs[states : states + columns.shape[1]]
    first = mine == 0
    turned = jnp.concatenate([jnp.where(first, a, b), jnp.where(first, b, a)], axis=0)
    turned = jnp.broadcast_to(turned[None], (chips,) + turned.shape)
    ones = theirs[states + columns.shape[1] :][: flags.shape[1]]
    all_flags[...] = jnp.concatenate([flags[mine], ones], axis=0)
    chunks[...] = jnp.concatenate([total.reshape(chips, -1, states), turned], axis=1).astype(BF16)


def rows_kernel(received, rows_in, packed, sums, chunks):
    g, d, p = rows_in[0], rows_in[1], rows_in[2]
    count, states = g.shape
    h = jnp.sum(received[:, :count, :].astype(F32), axis=0)
    y = h / p
    high = y.astype(BF16).astype(F32)
    middle = (y - high).astype(BF16).astype(F32)
    packed[:states, :] = received[:, count:, :].reshape(states, states)
    packed[states:, :] = jnp.concatenate([high, middle, y - high - middle], axis=0).astype(BF16)
    chunks[...] = jnp.broadcast_to(y[None].astype(BF16), chunks.shape)
    pairs = ((g, g), (g, h), (g, d), (d, d), (g, y), (d, y), (y, y), (h, y))
    sums[...] = jnp.concatenate([jnp.sum(a * b, axis=0, keepdims=True) for a, b in pairs], axis=0)


def renorm_kernel(left, operators, packed, packed_theirs, out, state_y):
    mine = lax.axis_index("core")
    first = mine == 0
    states = left.shape[2]
    a, b = packed[...].astype(F32), packed_theirs[...].astype(F32)
    count = state_y.shape[1]
    y = []
    for x in (a, b):
        terms = [x[i : i + count] for i in range(states, x.shape[0], count)]
        terms = terms[0::2], terms[1::2]
        low, high = [c[0] + c[1] + c[2] for c in terms]
        y.append(jnp.where(first, low, high))
    state_y[mine] = y[0]
    state_y[1 - mine] = y[1]
    for s, turned, blocks in ((mine, a[:states], left), (1 - mine, b[:states], operators.at[0])):
        rotation = jnp.transpose(turned).astype(BF16)
        turned = turned.astype(BF16)
        for k in range(blocks.shape[0]):
            rotated = dot(blocks[k], rotation).astype(BF16)
            out[k, s] = dot(turned, rotated).astype(BF16)


def dots_kernel(flags, gathered, left, right, swapped, level, row_sums, out):
    y = gathered[...].reshape(level.shape)
    states = y.shape[1]
    images = chip_image(jnp.concatenate([y, level[...].astype(BF16)], axis=1), flags, left, right, swapped)
    image = images[:states]
    d_hd = jnp.sum(level[...] * images[states:], axis=0, keepdims=True)
    y_hy = jnp.sum(y.astype(F32) * image, axis=0, keepdims=True)
    d_hy = jnp.sum(level[...] * image, axis=0, keepdims=True)
    rest = jnp.zeros((5, y.shape[1]), F32)
    sums = jnp.concatenate([row_sums[...], y_hy, d_hy, d_hd, rest], axis=0)
    sums = jnp.sum(sums, axis=1, keepdims=True)
    extent = (sums.shape[0], out.shape[1])
    here = lax.broadcasted_iota(jnp.int32, extent, 0) == lax.broadcasted_iota(jnp.int32, extent, 1)
    line = jnp.sum(jnp.where(here, sums, 0.0), axis=0, keepdims=True)
    out[...] = jnp.broadcast_to(line, out.shape)


def state_kernel(entries, received, state_rows, state_y, state, energy_out):
    sums = jnp.sum(received[...], axis=0, keepdims=True)
    extent = (16, sums.shape[1])
    here = lax.broadcasted_iota(jnp.int32, extent, 0) == lax.broadcasted_iota(jnp.int32, extent, 1)
    sums = jnp.sum(jnp.where(here, jnp.broadcast_to(sums, extent), 0.0), axis=1, keepdims=True)
    sums = jnp.broadcast_to(sums, (extent[0], state.shape[2]))
    gg, gh, gd, dd, gy, dy, yy, hy, y_hy, d_hy, d_hd = [sums[i : i + 1] for i in range(11)]
    inverse = 1.0 / entries
    first_square = 1.0 / (gg * inverse + 1e-06)
    rho = first_square * gh * inverse
    kappa = first_square * (gy - rho * gd) * inverse
    qq = yy - 2.0 * rho * dy + rho * rho * dd - 2.0 * kappa * (gy - rho * gd) + kappa * kappa * gg
    hq = hy - rho * gy - kappa * gh
    q_hq = y_hy - 2.0 * rho * d_hy + rho * rho * d_hd - 2.0 * kappa * (hy - rho * gy) + kappa * kappa * gh
    second_square = 1.0 / (first_square * qq * inverse + 1e-06)
    second_scale = jnp.sqrt(second_square)
    first_scale = jnp.sqrt(first_square)
    coupling = second_scale * first_square * hq * inverse
    rho_second = second_square * first_square * q_hq * inverse
    half_gap = (rho - rho_second) * 0.5
    energy = (rho + rho_second) * 0.5 - jnp.sqrt(half_gap * half_gap + coupling * coupling)
    weight_first = rho_second - energy
    weight_second = -coupling
    scaling = 1.0 / jnp.sqrt(weight_first * weight_first + weight_second * weight_second)
    on_second = weight_second * second_scale * scaling * first_scale
    on_first = weight_first * scaling * first_scale
    energy_out[...] = energy[:, : energy_out.shape[1]]
    g, d, y = state_rows[0], state_rows[1], state_y[...]
    state[...] = on_first[None] * g + on_second[None] * (y - rho[None] * d - kappa[None] * g)


def call(kernel, out_shape, in_specs, flops=0, scratch=(), limit=16):
    return pl.pallas_call(
        kernel,
        out_shape=out_shape,
        in_specs=in_specs,
        out_specs=jax.tree.map(lambda _: VMEM, out_shape),
        scratch_shapes=scratch,
        cost_estimate=pl.CostEstimate(flops=flops, bytes_accessed=1 << 20, transcendentals=0),
        compiler_params=pltpu.CompilerParams(vmem_limit_bytes=limit << 20),
    )


def local(left_hbm, right_hbm, pattern, guess_hbm, precond_hbm, rotation):
    ops, sectors, states = left_hbm.shape[:3]
    chips, cores, zones = (lax.axis_size(axis) for axis in ("chip", "core", "sec"))
    count = states // chips
    entries = float(sectors * zones * states * states)
    shape = jax.ShapeDtypeStruct
    dma = pltpu.SemaphoreType.DMA
    block = (states, states)
    flops = 4 * ops * sectors * states**3
    pattern = jnp.swapaxes(pattern, 0, 1)
    columns = jnp.swapaxes(rotation, 1, 2)

    def in_hbm(x):
        return pltpu.with_memory_space_constraint(x, pltpu.HBM)

    def swap(x):
        return lax.ppermute(x, "core", SWAP)

    operators = shape((ops,) + block, BF16)
    part, left, right, others, guess, precond, rows_other, columns, flags = call(
        other_kernel,
        (
            shape((states + 16, states), BF16),
            operators,
            operators,
            shape((2, ops) + block, BF16),
            shape(guess_hbm.shape, F32),
            shape(block, F32),
            shape((count // cores, states), F32),
            shape(columns.shape, BF16),
            shape((sectors, ops, states), F32),
        ),
        [HBM] * 6,
        flops // 2,
        [pltpu.SMEM(pattern.shape, jnp.int32), dma, dma, dma, dma((2,)), dma((2,)), dma((2,)), dma],
    )(*(in_hbm(x) for x in (pattern, left_hbm, right_hbm, guess_hbm, precond_hbm, columns)))
    theirs = swap(part)
    own, level, own_rows, state_rows = call(
        own_kernel,
        (
            shape(block, F32),
            shape(block, F32),
            shape((3, count, states), F32),
            shape((2, sectors, count // cores, states), F32),
        ),
        [VMEM] * 6,
        flops // 2,
    )(flags, left, right, guess, precond, rows_other)
    chunks, flags = call(
        chunks_kernel,
        (shape((chips, 2 * count, states), BF16), shape((2 * ops, states), F32)),
        [VMEM] * 4,
    )(own, theirs, columns, flags)
    received = lax.all_to_all(chunks, "chip", 0, 0)
    received, others = lax.optimization_barrier((received, others))
    swapped = swap(others)
    packed, row_sums, chunks = call(
        rows_kernel,
        (shape((states + 3 * count, states), BF16), shape((8, states), F32), shape((chips, count, states), BF16)),
        [VMEM] * 2,
    )(received, own_rows)
    gathered = lax.all_to_all(chunks, "chip", 0, 0)
    sums = call(dots_kernel, shape((chips * cores * zones, 128), F32), [VMEM] * 7, flops)(
        flags, gathered, left, right, swapped, level, row_sums
    )
    sums, packed = lax.optimization_barrier((sums, packed))
    sums = lax.all_to_all(sums, OPS + ("sec",), 0, 0)
    renormalized, state_y = call(
        renorm_kernel,
        (shape(left_hbm.shape, BF16), shape((sectors, count // cores, states), F32)),
        [VMEM] * 4,
        2 * flops,
    )(left, others, packed, swap(packed))
    new_state, energy = call(
        lambda *refs: state_kernel(entries, *refs),
        (shape((sectors, count // cores, states), F32), shape((1, 128), F32)),
        [VMEM] * 3,
    )(sums, state_rows, state_y)
    return new_state, energy[0, :1], renormalized


def solution(mesh):
    cores = 2
    mesh = Mesh(mesh.devices.reshape(-1, cores, mesh.shape["sec"]), ("chip", "core", "sec"))
    return jax.shard_map(
        local,
        mesh=mesh,
        in_specs=(
            P(OPS, "sec", None, None),
            P(OPS, "sec", None, None),
            P(OPS, "sec"),
            P("sec", None, None),
            P("sec", None, None),
            P("sec", None, OPS),
        ),
        out_specs=(P("sec", OPS, None), P(), P(OPS, "sec", None, None)),
        check_vma=False,
    )
```

```python
import jax
import jax.numpy as jnp
from jax import lax
from jax.experimental import pallas as pl
from jax.experimental.pallas import tpu as pltpu
from jax.sharding import Mesh, PartitionSpec as P

F32 = jnp.float32
BF16 = jnp.bfloat16
OPS = ("chip", "core")
SWAP = [(0, 1), (1, 0)]
VMEM = pl.BlockSpec(memory_space=pltpu.VMEM)
SMEM = pl.BlockSpec(memory_space=pltpu.SMEM)
HBM = pl.BlockSpec(memory_space=pltpu.HBM)


def dot(a, b):
    return jnp.dot(a, b, preferred_element_type=F32)


def image_of(x, left, right, flags):
    count, states = left.shape[:2]
    terms = x.shape[0] // states
    halves = []
    for k in range(count):
        block = left[k]
        half = dot(jnp.concatenate([block] * terms, axis=1), x).astype(BF16)
        parts = [half[:, i : i + states] for i in range(0, half.shape[1], states)]
        halves.append(jnp.concatenate(parts, axis=0) * flags[k : k + 1, :].astype(BF16))
    return dot(jnp.concatenate(halves, axis=1), right[...].reshape(count * states, states))


def chip_image(x, flags, left, right, swapped):
    count = left.shape[0]
    own = image_of(x, left, right, flags.at[pl.ds(0, count)])
    return own + image_of(x, swapped.at[0], swapped.at[1], flags.at[pl.ds(count, count)])


def two_terms(x):
    high = x.astype(BF16)
    return jnp.concatenate([high, (x - high.astype(F32)).astype(BF16)], axis=0)


def columns_of(columns, s):
    both = columns[...].astype(F32)
    count = both.shape[0] // 2
    return jnp.where(s == 0, both[:count], both[count:])


def other_kernel(
    pattern_hbm, left_hbm, right_hbm, guess_hbm, precond_hbm, columns_hbm,
    part, left, right, operators, guess, precond, rows_other, columns, flags,
    pattern, pattern_sem, columns_sem, rows_sem, guess_sem, left_sem, right_sem, precond_sem,
):
    mine, chip = lax.axis_index("core"), lax.axis_index("chip")
    other = 1 - mine
    count = rows_other.shape[0]
    own = pl.ds(pl.multiple_of((chip * 2 + mine) * count, count), count)
    small = [
        pltpu.make_async_copy(pattern_hbm, pattern, pattern_sem),
        pltpu.make_async_copy(columns_hbm, columns, columns_sem),
    ]
    copies = []
    for i, (s, l, r) in enumerate(((other, operators.at[0], operators.at[1]), (mine, left, right))):
        copies.append(
            [
                pltpu.make_async_copy(guess_hbm.at[s], guess.at[s], guess_sem.at[i]),
                pltpu.make_async_copy(left_hbm.at[:, s], l, left_sem.at[i]),
                pltpu.make_async_copy(right_hbm.at[:, s], r, right_sem.at[i]),
            ]
        )
    last = [
        pltpu.make_async_copy(precond_hbm.at[mine], precond, precond_sem),
        pltpu.make_async_copy(precond_hbm.at[other, own], rows_other, rows_sem),
    ]
    for copy in small + copies[0] + copies[1] + last:
        copy.start()
    for copy in small:
        copy.wait()
    for s in range(flags.shape[0]):
        for k in range(flags.shape[1]):
            flags[s, pl.ds(k, 1), :] = jnp.full((1, flags.shape[2]), pattern[s, k].astype(F32))
    turned = columns_of(columns, other)
    ones = flags[other]
    rest = jnp.zeros((part.shape[0] - guess.shape[1] - turned.shape[0] - ones.shape[0], turned.shape[1]), F32)
    for copy in copies[0]:
        copy.wait()
    image = image_of(two_terms(guess[other]), operators.at[0], operators.at[1], flags.at[other])
    part[...] = jnp.concatenate([image, turned, ones, rest], axis=0).astype(BF16)
    for copy in copies[1] + last:
        copy.wait()


def own_kernel(flags, left, right, guess, precond, rows_other, part, level, rows_out, state_rows):
    mine, chip = lax.axis_index("core"), lax.axis_index("chip")
    other = 1 - mine
    part[...] = image_of(two_terms(guess[mine]), left, right, flags.at[mine])
    level[...] = guess[mine] / precond[...]
    count = rows_out.shape[1]
    own = pl.ds(pl.multiple_of(chip * count, count), count)
    rows_out[0] = guess[mine, own, :]
    rows_out[1] = level[own, :]
    rows_out[2] = precond[own, :]
    count = state_rows.shape[2]
    own = pl.ds(pl.multiple_of((chip * 2 + mine) * count, count), count)
    state_rows[0, mine] = guess[mine, own, :]
    state_rows[1, mine] = level[own, :]
    state_rows[0, other] = guess[other, own, :]
    state_rows[1, other] = guess[other, own, :] / rows_other[...]


def chunks_kernel(own, theirs, columns, flags, chunks, all_flags):
    mine = lax.axis_index("core")
    chips, count, states = chunks.shape
    theirs = theirs[...].astype(F32)
    total = own[...] + theirs[:states]
    a = columns_of(columns, mine)
    b = theirs[states : states + a.shape[0]]
    first = mine == 0
    turned = jnp.concatenate([jnp.where(first, a, b), jnp.where(first, b, a)], axis=0)
    turned = jnp.broadcast_to(turned[None], (chips,) + turned.shape)
    ones = theirs[states + a.shape[0] :][: flags.shape[1]]
    all_flags[...] = jnp.concatenate([flags[mine], ones], axis=0)
    chunks[...] = jnp.concatenate([total.reshape(chips, -1, states), turned], axis=1).astype(BF16)


def rows_kernel(received, rows_in, packed, sums, chunks):
    g, d, p = rows_in[0], rows_in[1], rows_in[2]
    count, states = g.shape
    h = jnp.sum(received[:, :count, :].astype(F32), axis=0)
    y = h / p
    high = y.astype(BF16).astype(F32)
    middle = (y - high).astype(BF16).astype(F32)
    packed[:states, :] = received[:, count:, :].reshape(states, states)
    packed[states:, :] = jnp.concatenate([high, middle, y - high - middle], axis=0).astype(BF16)
    chunks[...] = jnp.broadcast_to(y[None].astype(BF16), chunks.shape)
    pairs = ((g, g), (g, h), (g, d), (d, d), (g, y), (d, y), (y, y), (h, y))
    sums[...] = jnp.concatenate([jnp.sum(a * b, axis=0, keepdims=True) for a, b in pairs], axis=0)


def renorm_kernel(left, operators, packed, packed_theirs, out, state_y):
    mine = lax.axis_index("core")
    first = mine == 0
    states = left.shape[2]
    a, b = packed[...].astype(F32), packed_theirs[...].astype(F32)
    count = state_y.shape[1]
    y = []
    for x in (a, b):
        terms = [x[i : i + count] for i in range(states, x.shape[0], count)]
        terms = terms[0::2], terms[1::2]
        low, high = [c[0] + c[1] + c[2] for c in terms]
        y.append(jnp.where(first, low, high))
    state_y[mine] = y[0]
    state_y[1 - mine] = y[1]
    for s, turned, blocks in ((mine, a[:states], left), (1 - mine, b[:states], operators.at[0])):
        rotation = jnp.transpose(turned).astype(BF16)
        turned = turned.astype(BF16)
        for k in range(blocks.shape[0]):
            rotated = dot(blocks[k], rotation).astype(BF16)
            out[k, s] = dot(turned, rotated).astype(BF16)


def dots_kernel(flags, gathered, left, right, swapped, level, row_sums, out):
    y = gathered[...].reshape(level.shape)
    states = y.shape[1]
    images = chip_image(jnp.concatenate([y, level[...].astype(BF16)], axis=1), flags, left, right, swapped)
    image = images[:states]
    d_hd = jnp.sum(level[...] * images[states:], axis=0, keepdims=True)
    y_hy = jnp.sum(y.astype(F32) * image, axis=0, keepdims=True)
    d_hy = jnp.sum(level[...] * image, axis=0, keepdims=True)
    rest = jnp.zeros((5, y.shape[1]), F32)
    sums = jnp.concatenate([row_sums[...], y_hy, d_hy, d_hd, rest], axis=0)
    sums = jnp.sum(sums, axis=1, keepdims=True)
    extent = (sums.shape[0], out.shape[1])
    here = lax.broadcasted_iota(jnp.int32, extent, 0) == lax.broadcasted_iota(jnp.int32, extent, 1)
    line = jnp.sum(jnp.where(here, sums, 0.0), axis=0, keepdims=True)
    out[...] = jnp.broadcast_to(line, out.shape)


def state_kernel(entries, received, state_rows, state_y, state, energy_out):
    sums = jnp.sum(received[...], axis=0, keepdims=True)
    extent = (16, sums.shape[1])
    here = lax.broadcasted_iota(jnp.int32, extent, 0) == lax.broadcasted_iota(jnp.int32, extent, 1)
    sums = jnp.sum(jnp.where(here, jnp.broadcast_to(sums, extent), 0.0), axis=1, keepdims=True)
    sums = jnp.broadcast_to(sums, (extent[0], state.shape[2]))
    gg, gh, gd, dd, gy, dy, yy, hy, y_hy, d_hy, d_hd = [sums[i : i + 1] for i in range(11)]
    inverse = 1.0 / entries
    first_square = 1.0 / (gg * inverse + 1e-06)
    rho = first_square * gh * inverse
    kappa = first_square * (gy - rho * gd) * inverse
    qq = yy - 2.0 * rho * dy + rho * rho * dd - 2.0 * kappa * (gy - rho * gd) + kappa * kappa * gg
    hq = hy - rho * gy - kappa * gh
    q_hq = y_hy - 2.0 * rho * d_hy + rho * rho * d_hd - 2.0 * kappa * (hy - rho * gy) + kappa * kappa * gh
    second_square = 1.0 / (first_square * qq * inverse + 1e-06)
    second_scale = jnp.sqrt(second_square)
    first_scale = jnp.sqrt(first_square)
    coupling = second_scale * first_square * hq * inverse
    rho_second = second_square * first_square * q_hq * inverse
    half_gap = (rho - rho_second) * 0.5
    energy = (rho + rho_second) * 0.5 - jnp.sqrt(half_gap * half_gap + coupling * coupling)
    weight_first = rho_second - energy
    weight_second = -coupling
    scaling = 1.0 / jnp.sqrt(weight_first * weight_first + weight_second * weight_second)
    on_second = weight_second * second_scale * scaling * first_scale
    on_first = weight_first * scaling * first_scale
    energy_out[...] = energy[:, : energy_out.shape[1]]
    g, d, y = state_rows[0], state_rows[1], state_y[...]
    state[...] = on_first[None] * g + on_second[None] * (y - rho[None] * d - kappa[None] * g)


def call(kernel, out_shape, in_specs, flops=0, scratch=(), limit=16):
    return pl.pallas_call(
        kernel,
        out_shape=out_shape,
        in_specs=in_specs,
        out_specs=jax.tree.map(lambda _: VMEM, out_shape),
        scratch_shapes=scratch,
        cost_estimate=pl.CostEstimate(flops=flops, bytes_accessed=1 << 20, transcendentals=0),
        compiler_params=pltpu.CompilerParams(vmem_limit_bytes=limit << 20),
    )


def local(left_hbm, right_hbm, pattern, guess_hbm, precond_hbm, rotation):
    ops, sectors, states = left_hbm.shape[:3]
    chips, cores, zones = (lax.axis_size(axis) for axis in ("chip", "core", "sec"))
    count = states // chips
    entries = float(sectors * zones * states * states)
    shape = jax.ShapeDtypeStruct
    dma = pltpu.SemaphoreType.DMA
    block = (states, states)
    flops = 4 * ops * sectors * states**3
    pattern = jnp.swapaxes(pattern, 0, 1)
    columns = jnp.swapaxes(rotation, 1, 2).reshape(-1, states)

    def in_hbm(x):
        return pltpu.with_memory_space_constraint(x, pltpu.HBM)

    def swap(x):
        return lax.ppermute(x, "core", SWAP)

    operators = shape((ops,) + block, BF16)
    part, left, right, others, guess, precond, rows_other, columns, flags = call(
        other_kernel,
        (
            shape((states + 16, states), BF16),
            operators,
            operators,
            shape((2, ops) + block, BF16),
            shape(guess_hbm.shape, F32),
            shape(block, F32),
            shape((count // cores, states), F32),
            shape(columns.shape, BF16),
            shape((sectors, ops, states), F32),
        ),
        [HBM] * 6,
        flops // 2,
        [pltpu.SMEM(pattern.shape, jnp.int32), dma, dma, dma, dma((2,)), dma((2,)), dma((2,)), dma],
    )(*(in_hbm(x) for x in (pattern, left_hbm, right_hbm, guess_hbm, precond_hbm, columns)))
    theirs = swap(part)
    own, level, own_rows, state_rows = call(
        own_kernel,
        (
            shape(block, F32),
            shape(block, F32),
            shape((3, count, states), F32),
            shape((2, sectors, count // cores, states), F32),
        ),
        [VMEM] * 6,
        flops // 2,
    )(flags, left, right, guess, precond, rows_other)
    chunks, flags = call(
        chunks_kernel,
        (shape((chips, 2 * count, states), BF16), shape((2 * ops, states), F32)),
        [VMEM] * 4,
    )(own, theirs, columns, flags)
    received = lax.all_to_all(chunks, "chip", 0, 0)
    received, others = lax.optimization_barrier((received, others))
    swapped = swap(others)
    packed, row_sums, chunks = call(
        rows_kernel,
        (shape((states + 3 * count, states), BF16), shape((8, states), F32), shape((chips, count, states), BF16)),
        [VMEM] * 2,
    )(received, own_rows)
    gathered = lax.all_to_all(chunks, "chip", 0, 0)
    sums = call(dots_kernel, shape((chips * cores * zones, 128), F32), [VMEM] * 7, flops)(
        flags, gathered, left, right, swapped, level, row_sums
    )
    sums, packed = lax.optimization_barrier((sums, packed))
    sums = lax.all_to_all(sums, OPS + ("sec",), 0, 0)
    renormalized, state_y = call(
        renorm_kernel,
        (shape(left_hbm.shape, BF16), shape((sectors, count // cores, states), F32)),
        [VMEM] * 4,
        2 * flops,
    )(left, others, packed, swap(packed))
    new_state, energy = call(
        lambda *refs: state_kernel(entries, *refs),
        (shape((sectors, count // cores, states), F32), shape((1, 128), F32)),
        [VMEM] * 3,
    )(sums, state_rows, state_y)
    return new_state, energy[0, :1], renormalized


def solution(mesh):
    cores = 2
    mesh = Mesh(mesh.devices.reshape(-1, cores, mesh.shape["sec"]), ("chip", "core", "sec"))
    return jax.shard_map(
        local,
        mesh=mesh,
        in_specs=(
            P(OPS, "sec", None, None),
            P(OPS, "sec", None, None),
            P(OPS, "sec"),
            P("sec", None, None),
            P("sec", None, None),
            P("sec", None, OPS),
        ),
        out_specs=(P("sec", OPS, None), P(), P(OPS, "sec", None, None)),
        check_vma=False,
    )
```

```python
import jax
import jax.numpy as jnp
from jax import lax
from jax.experimental import pallas as pl
from jax.experimental.pallas import tpu as pltpu
from jax.sharding import Mesh, PartitionSpec as P

F32 = jnp.float32
BF16 = jnp.bfloat16
OPS = ("chip", "core")
SWAP = [(0, 1), (1, 0)]
VMEM = pl.BlockSpec(memory_space=pltpu.VMEM)
SMEM = pl.BlockSpec(memory_space=pltpu.SMEM)
HBM = pl.BlockSpec(memory_space=pltpu.HBM)


def dot(a, b):
    return jnp.dot(a, b, preferred_element_type=F32)


def image_of(x, left, right, flags):
    count, states = left.shape[:2]
    terms = x.shape[0] // states
    halves = []
    for k in range(count):
        block = left[k]
        half = dot(jnp.concatenate([block] * terms, axis=1), x).astype(BF16)
        parts = [half[:, i : i + states] for i in range(0, half.shape[1], states)]
        halves.append(jnp.concatenate(parts, axis=0) * flags[k : k + 1, :].astype(BF16))
    return dot(jnp.concatenate(halves, axis=1), right[...].reshape(count * states, states))


def chip_image(x, flags, left, right, swapped):
    count = left.shape[0]
    own = image_of(x, left, right, flags.at[pl.ds(0, count)])
    return own + image_of(x, swapped.at[0], swapped.at[1], flags.at[pl.ds(count, count)])


def two_terms(x):
    high = x.astype(BF16)
    return jnp.concatenate([high, (x - high.astype(F32)).astype(BF16)], axis=0)


def columns_of(columns, s):
    both = columns[...].astype(F32)
    count = both.shape[0] // 2
    return jnp.where(s == 0, both[:count], both[count:])


def other_kernel(
    pattern_hbm, left_hbm, right_hbm, guess_hbm, precond_hbm, columns_hbm,
    part, left, right, operators, guess, precond, columns, flags,
    pattern, pattern_sem, columns_sem, guess_sem, left_sem, right_sem, precond_sem,
):
    mine = lax.axis_index("core")
    other = 1 - mine
    small = [
        pltpu.make_async_copy(pattern_hbm, pattern, pattern_sem),
        pltpu.make_async_copy(columns_hbm, columns, columns_sem),
    ]
    copies = []
    for i, (s, l, r) in enumerate(((other, operators.at[0], operators.at[1]), (mine, left, right))):
        copies.append(
            [
                pltpu.make_async_copy(guess_hbm.at[s], guess.at[s], guess_sem.at[i]),
                pltpu.make_async_copy(left_hbm.at[:, s], l, left_sem.at[i]),
                pltpu.make_async_copy(right_hbm.at[:, s], r, right_sem.at[i]),
            ]
        )
    last = [pltpu.make_async_copy(precond_hbm, precond, precond_sem)]
    for copy in copies[0] + small + copies[1] + last:
        copy.start()
    for copy in small:
        copy.wait()
    for s in range(flags.shape[0]):
        for k in range(flags.shape[1]):
            flags[s, pl.ds(k, 1), :] = jnp.full((1, flags.shape[2]), pattern[s, k].astype(F32))
    turned = columns_of(columns, other)
    ones = flags[other]
    rest = jnp.zeros((part.shape[0] - guess.shape[1] - turned.shape[0] - ones.shape[0], turned.shape[1]), F32)
    for copy in copies[0]:
        copy.wait()
    image = image_of(two_terms(guess[other]), operators.at[0], operators.at[1], flags.at[other])
    part[...] = jnp.concatenate([image, turned, ones, rest], axis=0).astype(BF16)
    for copy in copies[1] + last:
        copy.wait()


def own_kernel(flags, left, right, operators, guess, precond, part, level, rows_out, state_rows, d_hd):
    mine, chip = lax.axis_index("core"), lax.axis_index("chip")
    other = 1 - mine
    part[...] = image_of(two_terms(guess[mine]), left, right, flags.at[mine])
    level[...] = guess[...] / precond[...]
    dots = []
    for s, l, r in ((mine, left, right), (other, operators.at[0], operators.at[1])):
        d = level[s]
        image = image_of(d.astype(BF16), l, r, flags.at[s])
        dots.append(jnp.sum((d * image).reshape(-1, 8, d.shape[1]), axis=0))
    d_hd[...] = dots[0] + dots[1]
    count = rows_out.shape[1]
    own = pl.ds(pl.multiple_of(chip * count, count), count)
    for i, ref in enumerate((guess, level, precond)):
        rows_out[i] = ref[mine, own, :]
    count = state_rows.shape[2]
    own = pl.ds(pl.multiple_of((chip * 2 + mine) * count, count), count)
    for i, ref in enumerate((guess, level)):
        for s in range(ref.shape[0]):
            state_rows[i, s] = ref[s, own, :]


def chunks_kernel(own, theirs, columns, flags, chunks, all_flags):
    mine = lax.axis_index("core")
    chips, count, states = chunks.shape
    theirs = theirs[...].astype(F32)
    total = own[...] + theirs[:states]
    a = columns_of(columns, mine)
    b = theirs[states : states + a.shape[0]]
    first = mine == 0
    turned = jnp.concatenate([jnp.where(first, a, b), jnp.where(first, b, a)], axis=0)
    turned = jnp.broadcast_to(turned[None], (chips,) + turned.shape)
    ones = theirs[states + a.shape[0] :][: flags.shape[1]]
    all_flags[...] = jnp.concatenate([flags[mine], ones], axis=0)
    chunks[...] = jnp.concatenate([total.reshape(chips, -1, states), turned], axis=1).astype(BF16)


def rows_kernel(received, rows_in, packed, sums, chunks):
    g, d, p = rows_in[0], rows_in[1], rows_in[2]
    count, states = g.shape
    h = jnp.sum(received[:, :count, :].astype(F32), axis=0)
    y = h / p
    high = y.astype(BF16).astype(F32)
    middle = (y - high).astype(BF16).astype(F32)
    packed[:states, :] = received[:, count:, :].reshape(states, states)
    packed[states:, :] = jnp.concatenate([high, middle, y - high - middle], axis=0).astype(BF16)
    chunks[...] = jnp.broadcast_to(y[None].astype(BF16), chunks.shape)
    pairs = ((g, g), (g, h), (g, d), (d, d), (g, y), (d, y), (y, y), (h, y))
    sums[...] = jnp.concatenate([jnp.sum(a * b, axis=0, keepdims=True) for a, b in pairs], axis=0)


def renorm_kernel(left, operators, packed, packed_theirs, out, state_y):
    mine = lax.axis_index("core")
    first = mine == 0
    states = left.shape[2]
    a, b = packed[...].astype(F32), packed_theirs[...].astype(F32)
    count = state_y.shape[1]
    y = []
    for x in (a, b):
        terms = [x[i : i + count] for i in range(states, x.shape[0], count)]
        terms = terms[0::2], terms[1::2]
        low, high = [c[0] + c[1] + c[2] for c in terms]
        y.append(jnp.where(first, low, high))
    state_y[mine] = y[0]
    state_y[1 - mine] = y[1]
    for s, turned, blocks in ((mine, a[:states], left), (1 - mine, b[:states], operators.at[0])):
        rotation = jnp.transpose(turned).astype(BF16)
        turned = turned.astype(BF16)
        for k in range(blocks.shape[0]):
            rotated = dot(blocks[k], rotation).astype(BF16)
            out[k, s] = dot(turned, rotated).astype(BF16)


def dots_kernel(flags, gathered, left, right, swapped, level, row_sums, d_hd, out):
    d = level[lax.axis_index("core")]
    y = gathered[...].reshape(d.shape)
    image = chip_image(y, flags, left, right, swapped)
    dots = [jnp.sum((x * image).reshape(-1, 8, d.shape[1]), axis=0) for x in (y.astype(F32), d)]
    sums = jnp.sum(jnp.concatenate([row_sums[...]] + dots + [d_hd[...]], axis=0), axis=1, keepdims=True)
    extent = (sums.shape[0], out.shape[1])
    row, lane = (lax.broadcasted_iota(jnp.int32, extent, i) for i in range(2))
    here = jnp.where(row < 8, row, 7 + row // 8) == lane
    line = jnp.sum(jnp.where(here, sums, 0.0), axis=0, keepdims=True)
    out[...] = jnp.broadcast_to(line, out.shape)


def state_kernel(entries, received, state_rows, state_y, state, energy_out):
    sums = jnp.sum(received[...], axis=0, keepdims=True)
    extent = (16, sums.shape[1])
    here = lax.broadcasted_iota(jnp.int32, extent, 0) == lax.broadcasted_iota(jnp.int32, extent, 1)
    sums = jnp.sum(jnp.where(here, jnp.broadcast_to(sums, extent), 0.0), axis=1, keepdims=True)
    sums = jnp.broadcast_to(sums, (extent[0], state.shape[2]))
    gg, gh, gd, dd, gy, dy, yy, hy, y_hy, d_hy, d_hd = [sums[i : i + 1] for i in range(11)]
    inverse = 1.0 / entries
    first_square = 1.0 / (gg * inverse + 1e-06)
    rho = first_square * gh * inverse
    kappa = first_square * (gy - rho * gd) * inverse
    qq = yy - 2.0 * rho * dy + rho * rho * dd - 2.0 * kappa * (gy - rho * gd) + kappa * kappa * gg
    hq = hy - rho * gy - kappa * gh
    q_hq = y_hy - 2.0 * rho * d_hy + rho * rho * d_hd - 2.0 * kappa * (hy - rho * gy) + kappa * kappa * gh
    second_square = 1.0 / (first_square * qq * inverse + 1e-06)
    second_scale = jnp.sqrt(second_square)
    first_scale = jnp.sqrt(first_square)
    coupling = second_scale * first_square * hq * inverse
    rho_second = second_square * first_square * q_hq * inverse
    half_gap = (rho - rho_second) * 0.5
    energy = (rho + rho_second) * 0.5 - jnp.sqrt(half_gap * half_gap + coupling * coupling)
    weight_first = rho_second - energy
    weight_second = -coupling
    scaling = 1.0 / jnp.sqrt(weight_first * weight_first + weight_second * weight_second)
    on_second = weight_second * second_scale * scaling * first_scale
    on_first = weight_first * scaling * first_scale
    energy_out[...] = energy[:, : energy_out.shape[1]]
    g, d, y = state_rows[0], state_rows[1], state_y[...]
    state[...] = on_first[None] * g + on_second[None] * (y - rho[None] * d - kappa[None] * g)


def call(kernel, out_shape, in_specs, flops=0, scratch=(), limit=16):
    return pl.pallas_call(
        kernel,
        out_shape=out_shape,
        in_specs=in_specs,
        out_specs=jax.tree.map(lambda _: VMEM, out_shape),
        scratch_shapes=scratch,
        cost_estimate=pl.CostEstimate(flops=flops, bytes_accessed=1 << 20, transcendentals=0),
        compiler_params=pltpu.CompilerParams(vmem_limit_bytes=limit << 20),
    )


def local(left_hbm, right_hbm, pattern, guess_hbm, precond_hbm, rotation):
    ops, sectors, states = left_hbm.shape[:3]
    chips, cores, zones = (lax.axis_size(axis) for axis in ("chip", "core", "sec"))
    count = states // chips
    entries = float(sectors * zones * states * states)
    shape = jax.ShapeDtypeStruct
    dma = pltpu.SemaphoreType.DMA
    block = (states, states)
    flops = 4 * ops * sectors * states**3
    pattern = jnp.swapaxes(pattern, 0, 1)
    columns = jnp.swapaxes(rotation, 1, 2).reshape(-1, states)

    def in_hbm(x):
        return pltpu.with_memory_space_constraint(x, pltpu.HBM)

    def swap(x):
        return lax.ppermute(x, "core", SWAP)

    operators = shape((ops,) + block, BF16)
    part, left, right, others, guess, precond, columns, flags = call(
        other_kernel,
        (
            shape((states + 16, states), BF16),
            operators,
            operators,
            shape((2, ops) + block, BF16),
            shape(guess_hbm.shape, F32),
            shape(guess_hbm.shape, F32),
            shape(columns.shape, BF16),
            shape((sectors, ops, states), F32),
        ),
        [HBM] * 6,
        flops // 2,
        [pltpu.SMEM(pattern.shape, jnp.int32), dma, dma, dma((2,)), dma((2,)), dma((2,)), dma],
    )(*(in_hbm(x) for x in (pattern, left_hbm, right_hbm, guess_hbm, precond_hbm, columns)))
    theirs = swap(part)
    own, level, own_rows, state_rows, d_hd = call(
        own_kernel,
        (
            shape(block, F32),
            shape(guess.shape, F32),
            shape((3, count, states), F32),
            shape((2, sectors, count // cores, states), F32),
            shape((8, states), F32),
        ),
        [VMEM] * 6,
        flops // 2,
    )(flags, left, right, others, guess, precond)
    chunks, flags = call(
        chunks_kernel,
        (shape((chips, 2 * count, states), BF16), shape((2 * ops, states), F32)),
        [VMEM] * 4,
    )(own, theirs, columns, flags)
    received = lax.all_to_all(chunks, "chip", 0, 0)
    received, others = lax.optimization_barrier((received, others))
    swapped = swap(others)
    packed, row_sums, chunks = call(
        rows_kernel,
        (shape((states + 3 * count, states), BF16), shape((8, states), F32), shape((chips, count, states), BF16)),
        [VMEM] * 2,
    )(received, own_rows)
    gathered = lax.all_to_all(chunks, "chip", 0, 0)
    sums = call(dots_kernel, shape((chips * cores * zones, 128), F32), [VMEM] * 8, flops)(
        flags, gathered, left, right, swapped, level, row_sums, d_hd
    )
    sums, packed = lax.optimization_barrier((sums, packed))
    sums = lax.all_to_all(sums, OPS + ("sec",), 0, 0)
    renormalized, state_y = call(
        renorm_kernel,
        (shape(left_hbm.shape, BF16), shape((sectors, count // cores, states), F32)),
        [VMEM] * 4,
        2 * flops,
    )(left, others, packed, swap(packed))
    new_state, energy = call(
        lambda *refs: state_kernel(entries, *refs),
        (shape((sectors, count // cores, states), F32), shape((1, 128), F32)),
        [VMEM] * 3,
    )(sums, state_rows, state_y)
    return new_state, energy[0, :1], renormalized


def solution(mesh):
    cores = 2
    mesh = Mesh(mesh.devices.reshape(-1, cores, mesh.shape["sec"]), ("chip", "core", "sec"))
    return jax.shard_map(
        local,
        mesh=mesh,
        in_specs=(
            P(OPS, "sec", None, None),
            P(OPS, "sec", None, None),
            P(OPS, "sec"),
            P("sec", None, None),
            P("sec", None, None),
            P("sec", None, OPS),
        ),
        out_specs=(P("sec", OPS, None), P(), P(OPS, "sec", None, None)),
        check_vma=False,
    )
```

```python
import jax
import jax.numpy as jnp
from jax import lax
from jax.experimental import pallas as pl
from jax.experimental.pallas import tpu as pltpu
from jax.sharding import Mesh, PartitionSpec as P

F32 = jnp.float32
BF16 = jnp.bfloat16
OPS = ("chip", "core")
SWAP = [(0, 1), (1, 0)]
VMEM = pl.BlockSpec(memory_space=pltpu.VMEM)
SMEM = pl.BlockSpec(memory_space=pltpu.SMEM)
HBM = pl.BlockSpec(memory_space=pltpu.HBM)


def dot(a, b):
    return jnp.dot(a, b, preferred_element_type=F32)


def image_of(x, left, right, flags):
    count, states = left.shape[:2]
    terms = x.shape[0] // states
    halves = []
    for k in range(count):
        block = left[k]
        half = dot(jnp.concatenate([block] * terms, axis=1), x).astype(BF16)
        parts = [half[:, i : i + states] for i in range(0, half.shape[1], states)]
        halves.append(jnp.concatenate(parts, axis=0) * flags[k : k + 1, :].astype(BF16))
    return dot(jnp.concatenate(halves, axis=1), right[...].reshape(count * states, states))


def chip_image(x, flags, left, right, swapped):
    count = left.shape[0]
    own = image_of(x, left, right, flags.at[pl.ds(0, count)])
    return own + image_of(x, swapped.at[0], swapped.at[1], flags.at[pl.ds(count, count)])


def two_terms(x):
    high = x.astype(BF16)
    return jnp.concatenate([high, (x - high.astype(F32)).astype(BF16)], axis=0)


def columns_of(columns, s):
    both = columns[...].astype(F32)
    count = both.shape[0] // 2
    return jnp.where(s == 0, both[:count], both[count:])


def other_kernel(
    pattern_hbm, left_hbm, right_hbm, guess_hbm, precond_hbm, columns_hbm,
    part, left, right, operators, guess, precond, rows_other, columns, flags,
    pattern, pattern_sem, columns_sem, rows_sem, guess_sem, left_sem, right_sem, precond_sem,
):
    mine, chip = lax.axis_index("core"), lax.axis_index("chip")
    other = 1 - mine
    count = rows_other.shape[0]
    own = pl.ds(pl.multiple_of((chip * 2 + mine) * count, count), count)
    small = [
        pltpu.make_async_copy(pattern_hbm, pattern, pattern_sem),
        pltpu.make_async_copy(columns_hbm, columns, columns_sem),
    ]
    copies = []
    for i, (s, l, r) in enumerate(((other, operators.at[0], operators.at[1]), (mine, left, right))):
        copies.append(
            [
                pltpu.make_async_copy(guess_hbm.at[s], guess.at[s], guess_sem.at[i]),
                pltpu.make_async_copy(left_hbm.at[:, s], l, left_sem.at[i]),
                pltpu.make_async_copy(right_hbm.at[:, s], r, right_sem.at[i]),
            ]
        )
    last = [
        pltpu.make_async_copy(precond_hbm.at[mine], precond, precond_sem),
        pltpu.make_async_copy(precond_hbm.at[other, own], rows_other, rows_sem),
    ]
    for copy in copies[0] + small + copies[1] + last:
        copy.start()
    for copy in small:
        copy.wait()
    for s in range(flags.shape[0]):
        for k in range(flags.shape[1]):
            flags[s, pl.ds(k, 1), :] = jnp.full((1, flags.shape[2]), pattern[s, k].astype(F32))
    turned = columns_of(columns, other)
    ones = flags[other]
    rest = jnp.zeros((part.shape[0] - guess.shape[1] - turned.shape[0] - ones.shape[0], turned.shape[1]), F32)
    for copy in copies[0]:
        copy.wait()
    image = image_of(two_terms(guess[other]), operators.at[0], operators.at[1], flags.at[other])
    part[...] = jnp.concatenate([image, turned, ones, rest], axis=0).astype(BF16)
    for copy in copies[1] + last:
        copy.wait()


def own_kernel(flags, left, right, guess, precond, rows_other, part, level, rows_out, state_rows):
    mine, chip = lax.axis_index("core"), lax.axis_index("chip")
    other = 1 - mine
    part[...] = image_of(two_terms(guess[mine]), left, right, flags.at[mine])
    level[...] = guess[mine] / precond[...]
    count = rows_out.shape[1]
    own = pl.ds(pl.multiple_of(chip * count, count), count)
    rows_out[0] = guess[mine, own, :]
    rows_out[1] = level[own, :]
    rows_out[2] = precond[own, :]
    count = state_rows.shape[2]
    own = pl.ds(pl.multiple_of((chip * 2 + mine) * count, count), count)
    state_rows[0, mine] = guess[mine, own, :]
    state_rows[1, mine] = level[own, :]
    state_rows[0, other] = guess[other, own, :]
    state_rows[1, other] = guess[other, own, :] / rows_other[...]


def chunks_kernel(own, theirs, columns, flags, chunks, all_flags):
    mine = lax.axis_index("core")
    chips, count, states = chunks.shape
    theirs = theirs[...].astype(F32)
    total = own[...] + theirs[:states]
    a = columns_of(columns, mine)
    b = theirs[states : states + a.shape[0]]
    first = mine == 0
    turned = jnp.concatenate([jnp.where(first, a, b), jnp.where(first, b, a)], axis=0)
    turned = jnp.broadcast_to(turned[None], (chips,) + turned.shape)
    ones = theirs[states + a.shape[0] :][: flags.shape[1]]
    all_flags[...] = jnp.concatenate([flags[mine], ones], axis=0)
    chunks[...] = jnp.concatenate([total.reshape(chips, -1, states), turned], axis=1).astype(BF16)


def rows_kernel(received, rows_in, packed, sums, chunks):
    g, d, p = rows_in[0], rows_in[1], rows_in[2]
    count, states = g.shape
    h = jnp.sum(received[:, :count, :].astype(F32), axis=0)
    y = h / p
    high = y.astype(BF16).astype(F32)
    middle = (y - high).astype(BF16).astype(F32)
    packed[:states, :] = received[:, count:, :].reshape(states, states)
    packed[states:, :] = jnp.concatenate([high, middle, y - high - middle], axis=0).astype(BF16)
    chunks[...] = jnp.broadcast_to(y[None].astype(BF16), chunks.shape)
    pairs = ((g, g), (g, h), (g, d), (d, d), (g, y), (d, y), (y, y), (h, y))
    sums[...] = jnp.concatenate([jnp.sum(a * b, axis=0, keepdims=True) for a, b in pairs], axis=0)


def renorm_kernel(left, operators, packed, packed_theirs, out, state_y):
    mine = lax.axis_index("core")
    first = mine == 0
    states = left.shape[2]
    a, b = packed[...].astype(F32), packed_theirs[...].astype(F32)
    count = state_y.shape[1]
    y = []
    for x in (a, b):
        terms = [x[i : i + count] for i in range(states, x.shape[0], count)]
        terms = terms[0::2], terms[1::2]
        low, high = [c[0] + c[1] + c[2] for c in terms]
        y.append(jnp.where(first, low, high))
    state_y[mine] = y[0]
    state_y[1 - mine] = y[1]
    for s, turned, blocks in ((mine, a[:states], left), (1 - mine, b[:states], operators.at[0])):
        rotation = jnp.transpose(turned).astype(BF16)
        turned = turned.astype(BF16)
        for k in range(blocks.shape[0]):
            rotated = dot(blocks[k], rotation).astype(BF16)
            out[k, s] = dot(turned, rotated).astype(BF16)


def dots_kernel(flags, gathered, left, right, swapped, level, row_sums, out):
    y = gathered[...].reshape(level.shape)
    states = y.shape[1]
    images = chip_image(jnp.concatenate([y, level[...].astype(BF16)], axis=1), flags, left, right, swapped)
    image = images[:states]
    d = level[...]
    pairs = ((y.astype(F32), image), (d, image), (d, images[states:]))
    dots = [jnp.sum((a * b).reshape(-1, 8, states), axis=0) for a, b in pairs]
    sums = jnp.sum(jnp.concatenate([row_sums[...]] + dots, axis=0), axis=1, keepdims=True)
    extent = (sums.shape[0], out.shape[1])
    row, lane = (lax.broadcasted_iota(jnp.int32, extent, i) for i in range(2))
    here = jnp.where(row < 8, row, 7 + row // 8) == lane
    line = jnp.sum(jnp.where(here, sums, 0.0), axis=0, keepdims=True)
    out[...] = jnp.broadcast_to(line, out.shape)


def state_kernel(entries, received, state_rows, state_y, state, energy_out):
    sums = jnp.sum(received[...], axis=0, keepdims=True)
    extent = (16, sums.shape[1])
    here = lax.broadcasted_iota(jnp.int32, extent, 0) == lax.broadcasted_iota(jnp.int32, extent, 1)
    sums = jnp.sum(jnp.where(here, jnp.broadcast_to(sums, extent), 0.0), axis=1, keepdims=True)
    sums = jnp.broadcast_to(sums, (extent[0], state.shape[2]))
    gg, gh, gd, dd, gy, dy, yy, hy, y_hy, d_hy, d_hd = [sums[i : i + 1] for i in range(11)]
    inverse = 1.0 / entries
    first_square = 1.0 / (gg * inverse + 1e-06)
    rho = first_square * gh * inverse
    kappa = first_square * (gy - rho * gd) * inverse
    qq = yy - 2.0 * rho * dy + rho * rho * dd - 2.0 * kappa * (gy - rho * gd) + kappa * kappa * gg
    hq = hy - rho * gy - kappa * gh
    q_hq = y_hy - 2.0 * rho * d_hy + rho * rho * d_hd - 2.0 * kappa * (hy - rho * gy) + kappa * kappa * gh
    second_square = 1.0 / (first_square * qq * inverse + 1e-06)
    second_scale = jnp.sqrt(second_square)
    first_scale = jnp.sqrt(first_square)
    coupling = second_scale * first_square * hq * inverse
    rho_second = second_square * first_square * q_hq * inverse
    half_gap = (rho - rho_second) * 0.5
    energy = (rho + rho_second) * 0.5 - jnp.sqrt(half_gap * half_gap + coupling * coupling)
    weight_first = rho_second - energy
    weight_second = -coupling
    scaling = 1.0 / jnp.sqrt(weight_first * weight_first + weight_second * weight_second)
    on_second = weight_second * second_scale * scaling * first_scale
    on_first = weight_first * scaling * first_scale
    energy_out[...] = energy[:, : energy_out.shape[1]]
    g, d, y = state_rows[0], state_rows[1], state_y[...]
    state[...] = on_first[None] * g + on_second[None] * (y - rho[None] * d - kappa[None] * g)


def call(kernel, out_shape, in_specs, flops=0, scratch=(), limit=16):
    return pl.pallas_call(
        kernel,
        out_shape=out_shape,
        in_specs=in_specs,
        out_specs=jax.tree.map(lambda _: VMEM, out_shape),
        scratch_shapes=scratch,
        cost_estimate=pl.CostEstimate(flops=flops, bytes_accessed=1 << 20, transcendentals=0),
        compiler_params=pltpu.CompilerParams(vmem_limit_bytes=limit << 20),
    )


def local(left_hbm, right_hbm, pattern, guess_hbm, precond_hbm, rotation):
    ops, sectors, states = left_hbm.shape[:3]
    chips, cores, zones = (lax.axis_size(axis) for axis in ("chip", "core", "sec"))
    count = states // chips
    entries = float(sectors * zones * states * states)
    shape = jax.ShapeDtypeStruct
    dma = pltpu.SemaphoreType.DMA
    block = (states, states)
    flops = 4 * ops * sectors * states**3
    pattern = jnp.swapaxes(pattern, 0, 1)
    columns = jnp.swapaxes(rotation, 1, 2).reshape(-1, states)

    def in_hbm(x):
        return pltpu.with_memory_space_constraint(x, pltpu.HBM)

    def swap(x):
        return lax.ppermute(x, "core", SWAP)

    operators = shape((ops,) + block, BF16)
    part, left, right, others, guess, precond, rows_other, columns, flags = call(
        other_kernel,
        (
            shape((states + 16, states), BF16),
            operators,
            operators,
            shape((2, ops) + block, BF16),
            shape(guess_hbm.shape, F32),
            shape(block, F32),
            shape((count // cores, states), F32),
            shape(columns.shape, BF16),
            shape((sectors, ops, states), F32),
        ),
        [HBM] * 6,
        flops // 2,
        [pltpu.SMEM(pattern.shape, jnp.int32), dma, dma, dma, dma((2,)), dma((2,)), dma((2,)), dma],
    )(*(in_hbm(x) for x in (pattern, left_hbm, right_hbm, guess_hbm, precond_hbm, columns)))
    theirs = swap(part)
    own, level, own_rows, state_rows = call(
        own_kernel,
        (
            shape(block, F32),
            shape(block, F32),
            shape((3, count, states), F32),
            shape((2, sectors, count // cores, states), F32),
        ),
        [VMEM] * 6,
        flops // 2,
    )(flags, left, right, guess, precond, rows_other)
    chunks, flags = call(
        chunks_kernel,
        (shape((chips, 2 * count, states), BF16), shape((2 * ops, states), F32)),
        [VMEM] * 4,
    )(own, theirs, columns, flags)
    received = lax.all_to_all(chunks, "chip", 0, 0)
    received, others = lax.optimization_barrier((received, others))
    swapped = swap(others)
    packed, row_sums, chunks = call(
        rows_kernel,
        (shape((states + 3 * count, states), BF16), shape((8, states), F32), shape((chips, count, states), BF16)),
        [VMEM] * 2,
    )(received, own_rows)
    gathered = lax.all_to_all(chunks, "chip", 0, 0)
    sums = call(dots_kernel, shape((chips * cores * zones, 128), F32), [VMEM] * 7, flops)(
        flags, gathered, left, right, swapped, level, row_sums
    )
    sums, packed = lax.optimization_barrier((sums, packed))
    sums = lax.all_to_all(sums, OPS + ("sec",), 0, 0)
    renormalized, state_y = call(
        renorm_kernel,
        (shape(left_hbm.shape, BF16), shape((sectors, count // cores, states), F32)),
        [VMEM] * 4,
        2 * flops,
    )(left, others, packed, swap(packed))
    new_state, energy = call(
        lambda *refs: state_kernel(entries, *refs),
        (shape((sectors, count // cores, states), F32), shape((1, 128), F32)),
        [VMEM] * 3,
    )(sums, state_rows, state_y)
    return new_state, energy[0, :1], renormalized


def solution(mesh):
    cores = 2
    mesh = Mesh(mesh.devices.reshape(-1, cores, mesh.shape["sec"]), ("chip", "core", "sec"))
    return jax.shard_map(
        local,
        mesh=mesh,
        in_specs=(
            P(OPS, "sec", None, None),
            P(OPS, "sec", None, None),
            P(OPS, "sec"),
            P("sec", None, None),
            P("sec", None, None),
            P("sec", None, OPS),
        ),
        out_specs=(P("sec", OPS, None), P(), P(OPS, "sec", None, None)),
        check_vma=False,
    )
```
